32 devices in a mesh: tile: 8 (over y, x, core), dp: 4 (over z).
Axes of the slice: x: 2, y: 2, z: 4, core: 2. Of those that a mesh axis runs over, the one named last changes fastest.
Arguments:
- scan_pixels: bfloat16 [4, 20, 2048, 128], P('dp', None, 'tile'), may hold values from -6 to 6
- labels: int32 [4, 10, 2048], P('dp', None, 'tile'), may hold values from 0 to 7
- conv1_weight: bfloat16 [3, 192, 128], replicated, may hold values from -0.25 to 0.25
- conv2_weight: bfloat16 [3, 384, 256], replicated, may hold values from -0.1875 to 0.1875
- context_weight: bfloat16 [7, 1792, 256], replicated, may hold values from -0.0546875 to 0.0546875
- up_weight: bfloat16 [256, 128], replicated, may hold values from -0.375 to 0.375
- skip_weight: bfloat16 [128, 128], replicated, may hold values from -0.5 to 0.5
- class_weight: bfloat16 [8, 128], replicated, may hold values from -0.12374368670764582 to 0.12374368670764582
Outputs:
- logits: float32 [4, 8, 10, 2048], P('dp', None, None, 'tile')
- grad_features: float32 [4, 10, 2048, 128], P('dp', None, 'tile')
- grad_conv1: float32 [3, 192, 128], replicated
- grad_conv2: float32 [3, 384, 256], replicated
- grad_context: float32 [7, 1792, 256], replicated
- grad_up: float32 [256, 128], replicated
- grad_skip: float32 [128, 128], replicated
- grad_out: float32 [8, 128], replicated
The draws below stay inside these ranges and needn't reach their ends.
All inputs are finite; a program needn't handle non-finite values.
Results may differ from the reference program's by a relative error of at most 0.01.
Values may be sent and summed in bfloat16 or wider, within the bound.
No kernel may reach another device: no remote copies, remote signals or barrier semaphores. Data moves between devices by JAX's collectives and lax.ppermute only.
A program may use at most 128 MiB of HBM per device.

```python
import jax
import jax.numpy as jnp

CIN = 64
C1 = 128
C2 = 256
K = 8
COLUMN_SPREAD = 16
ROWS = 20
WIDTH = 4096
SLABS = 4
PIXELS = 81920


def draw_class_weight(key, part):
    key_base = jax.random.fold_in(key, 11)
    key_columns = jax.random.fold_in(key, 12)
    key_rows = jax.random.fold_in(key, 13)
    half_classes = K // 2
    half_channels = C1 // 2
    base_draw = jnp.clip(jax.random.normal(key_base, (half_classes, half_channels), jnp.float32), -2.0, 2.0)
    column_factor = 1.0 + 0.05 * jax.random.uniform(key_columns, (half_classes, half_channels), jnp.float32, -1.0, 1.0)
    row_factor = 1.0 + 0.05 * jax.random.uniform(key_rows, (half_classes, C1), jnp.float32, -1.0, 1.0)
    upper_rows = jnp.concatenate([base_draw, -base_draw * column_factor], axis=1)
    whole_table = jnp.concatenate([upper_rows, -upper_rows * row_factor], axis=0)
    scale_value = 0.7 * C1 ** (-0.5)
    limit_value = 2.0 * scale_value
    return jnp.clip(whole_table * scale_value, -limit_value, limit_value).astype(jnp.bfloat16)


def plant(result, stream_key, smallest, largest):
    index_at = [jax.random.randint(jax.random.fold_in(stream_key, axis), (), 0, length) for axis, length in enumerate(result.shape)]
    main_axis = result.shape.index(max(result.shape))
    next_to = index_at[:main_axis] + [(index_at[main_axis] + 1) % result.shape[main_axis]] + index_at[main_axis + 1:]
    return result.at[tuple(index_at)].set(smallest).at[tuple(next_to)].set(largest)


def block_levels(own_key, extent, pieces, smallest, high):
    gain, own = 1.0, jax.random.fold_in(own_key, 6)
    for axis_at, blocks in pieces:
        steps = jnp.exp(jax.random.uniform(jax.random.fold_in(own, axis_at), (blocks,), jnp.float32, smallest / len(pieces), high / len(pieces)))
        gain = gain * jnp.repeat(steps, extent[axis_at] // blocks).reshape([-1 if axis == axis_at else 1 for axis in range(len(extent))])
    return gain


def gaussian(own_key, shape, scale, bound, cuts=(), held_as=jnp.bfloat16):
    array = scale * jax.random.normal(own_key, shape, jnp.float32)
    if cuts:
        array = array * block_levels(own_key, shape, cuts, -0.22, 0.18)
    return jnp.clip(array, -bound, bound).astype(held_as)


def setup_inputs(seed: int = 0) -> dict:
    splits = jax.random.split(jax.random.key(seed), 9)
    scan_pixels = gaussian(splits[0], (SLABS, ROWS, WIDTH // 2, 2 * CIN), 1.0, 6.0, ((0, 4), (2, 8)))
    labels = plant(jax.random.randint(splits[1], (SLABS, ROWS // 2, WIDTH // 2), 0, K), jax.random.fold_in(splits[1], 1), 0, K - 1).astype(jnp.int32)
    conv1_weight = gaussian(splits[2], (3, 3 * CIN, C1), (9 * CIN) ** -0.5, 0.25)
    conv2_weight = gaussian(splits[3], (3, 3 * C1, C2), (9 * C1) ** -0.5, 0.1875)
    context_weight = gaussian(splits[4], (7, 7 * C2, C2), (49 * C2) ** -0.5, 0.0546875)
    up_weight = gaussian(splits[5], (C2, C1), C2 ** -0.5, 0.375)
    skip_weight = gaussian(splits[6], (C1, C1), C1 ** -0.5, 0.5)
    class_weight = draw_class_weight(jax.random.fold_in(splits[8], 71), 0)
    return dict(scan_pixels=scan_pixels, labels=labels, conv1_weight=conv1_weight, conv2_weight=conv2_weight, context_weight=context_weight, up_weight=up_weight, skip_weight=skip_weight, class_weight=class_weight)


def product(pattern, lhs_array, rhs_array):
    return jnp.einsum(pattern, lhs_array.astype(jnp.float32), rhs_array.astype(jnp.float32))

def silu_slope(inputs):
    sigmoid_value = jax.nn.sigmoid(inputs)
    return sigmoid_value + inputs * sigmoid_value * (1.0 - sigmoid_value)

def column_taps(feature_map, left_edge):
    channels = feature_map.shape[-1] // 2
    even_cols = feature_map[..., :channels]
    odd_cols = feature_map[..., channels:]
    before_cols = jnp.concatenate([left_edge, odd_cols[:, :-1]], axis=1)
    joined = jnp.concatenate([before_cols, even_cols, odd_cols], axis=-1)
    paired = joined.reshape(joined.shape[0] // 2, 2, joined.shape[1], joined.shape[2])
    row_even = paired[:, 0]
    row_odd = paired[:, 1]
    row_before = jnp.concatenate([jnp.zeros_like(row_odd[:1]), row_odd[:-1]], axis=0)
    return (row_before, row_even, row_odd)

def conv_apply(taps, weight):
    running = product('rwc,cd->rwd', taps[0], weight[0])
    for tap_index in range(1, 3):
        running = running + product('rwc,cd->rwd', taps[tap_index], weight[tap_index])
    return running

def conv_weight_grad(taps, gradient):
    return jnp.stack([product('rwc,rwd->cd', taps[tap_index], gradient) for tap_index in range(3)])

def taps_back(gradient, weight, channels):
    grad_taps = [product('rwd,cd->rwc', gradient, weight[tap_index]) for tap_index in range(3)]
    grad_before, grad_even, grad_odd = grad_taps
    grad_odd = grad_odd + jnp.concatenate([grad_before[1:], jnp.zeros_like(grad_before[:1])], axis=0)
    joined = jnp.stack([grad_even, grad_odd], axis=1)
    joined = joined.reshape(2 * grad_even.shape[0], grad_even.shape[1], grad_even.shape[2])
    col_before = joined[..., :channels]
    col_even = joined[..., channels:2 * channels]
    col_odd = joined[..., 2 * channels:]
    col_odd = col_odd + jnp.concatenate([col_before[:, 1:], jnp.zeros_like(col_before[:, :1])], axis=1)
    return (jnp.concatenate([col_even, col_odd], axis=-1), col_before[:, :1])

def context_taps(widened_map, slab_height, slab_width):
    bordered_map = jnp.pad(widened_map, ((3, 3), (0, 0), (0, 0)))
    return [jnp.concatenate([bordered_map[row_offset:row_offset + slab_height, column_offset * COLUMN_SPREAD:column_offset * COLUMN_SPREAD + slab_width] for column_offset in range(7)], axis=-1) for row_offset in range(7)]

def context_apply(stacks, weight):
    running = product('rwc,cd->rwd', stacks[0], weight[0])
    for row_offset in range(1, 7):
        running = running + product('rwc,cd->rwd', stacks[row_offset], weight[row_offset])
    return running

def context_back(widened_gradient, weight, slab_height, slab_width, channels):
    bordered_map = jnp.pad(widened_gradient, ((3, 3), (0, 0), (0, 0)))
    running = jnp.zeros((slab_height, slab_width, channels), jnp.float32)
    for row_offset in range(7):
        leading_row = 6 - row_offset
        picked_values = jnp.concatenate([bordered_map[leading_row:leading_row + slab_height, (6 - column_offset) * COLUMN_SPREAD:(6 - column_offset) * COLUMN_SPREAD + slab_width] for column_offset in range(7)], axis=-1)
        picked_values = picked_values.reshape(slab_height, slab_width, 7, channels)
        running = running + product('rwbd,bcd->rwc', picked_values, weight[row_offset].reshape(7, channels, channels))
    return running

def slab_pass(image_slab, label_slab, conv1_weight, conv2_weight, context_weight, up_weight, skip_weight, class_weight):
    channels_in = image_slab.shape[-1] // 2
    first_edge = jnp.zeros((image_slab.shape[0], 1, channels_in), jnp.bfloat16)
    first_taps = column_taps(image_slab, first_edge)
    first_pre = conv_apply(first_taps, conv1_weight)
    first_map = jax.nn.silu(first_pre).astype(jnp.bfloat16)
    half_rows, first_cols, width_one = first_map.shape
    second_field = first_map.reshape(half_rows, first_cols // 2, 2 * width_one)
    second_edge = jnp.zeros((half_rows, 1, width_one), jnp.bfloat16)
    second_taps = column_taps(second_field, second_edge)
    second_pre = conv_apply(second_taps, conv2_weight)
    later_feature_map = jax.nn.silu(second_pre).astype(jnp.bfloat16)
    slab_height, slab_width, width_two = later_feature_map.shape
    widened_map = jnp.pad(later_feature_map, ((0, 0), (3 * COLUMN_SPREAD, 3 * COLUMN_SPREAD), (0, 0)))
    stacks = context_taps(widened_map, slab_height, slab_width)
    context_pre = context_apply(stacks, context_weight)
    context = (later_feature_map.astype(jnp.float32) + jax.nn.silu(context_pre)).astype(jnp.bfloat16)
    coarse_mix = product('rwc,cd->rwd', context, up_weight)
    upsampled = jnp.broadcast_to(coarse_mix[:, None, :, None, :], (slab_height, 2, slab_width, 2, width_one)).reshape(half_rows, first_cols, width_one)
    decoder_pre = product('rwc,cd->rwd', first_map, skip_weight) + upsampled
    decoded = jax.nn.silu(decoder_pre).astype(jnp.bfloat16)
    logits = product('rwc,kc->krw', decoded, class_weight)
    target = (label_slab[None] == jnp.arange(K, dtype=jnp.int32)[:, None, None]).astype(jnp.float32)
    grad_logits = (jax.nn.sigmoid(logits) - target).astype(jnp.bfloat16)
    out_term = product('krw,rwc->kc', grad_logits, decoded)
    grad_decoded = product('krw,kc->rwc', grad_logits, class_weight)
    grad_decoder = (grad_decoded * silu_slope(decoder_pre)).astype(jnp.bfloat16)
    skip_term = product('rwc,rwd->cd', first_map, grad_decoder)
    pooled = grad_decoder.astype(jnp.float32).reshape(slab_height, 2, slab_width, 2, width_one).sum(axis=(1, 3)).astype(jnp.bfloat16)
    up_term = product('rwc,rwd->cd', context, pooled)
    grad_context_map = product('rwd,cd->rwc', pooled, up_weight)
    skip_features = product('rwd,cd->rwc', grad_decoder, skip_weight)
    context_input_gradient = (grad_context_map * silu_slope(context_pre)).astype(jnp.bfloat16)
    context_term = jnp.stack([product('rwc,rwd->cd', stacks[row_offset], context_input_gradient) for row_offset in range(7)])
    widened_gradient = jnp.pad(context_input_gradient, ((0, 0), (3 * COLUMN_SPREAD, 3 * COLUMN_SPREAD), (0, 0)))
    grad_second = grad_context_map + context_back(widened_gradient, context_weight, slab_height, slab_width, width_two)
    second_grad = (grad_second * silu_slope(second_pre)).astype(jnp.bfloat16)
    conv2_term = conv_weight_grad(second_taps, second_grad)
    grad_field, grad_edge = taps_back(second_grad, conv2_weight, width_one)
    grad_features = skip_features + grad_field.reshape(half_rows, first_cols, width_one)
    first_grad = (grad_features * silu_slope(first_pre)).astype(jnp.bfloat16)
    conv1_term = conv_weight_grad(first_taps, first_grad)
    return (logits, grad_features, (conv1_term, conv2_term, context_term, up_term, skip_term, out_term))

def reference(scan_pixels, labels, conv1_weight, conv2_weight, context_weight, up_weight, skip_weight, class_weight):
    logit_list = []
    feature_list = []
    totals = None
    for slab_index in range(SLABS):
        logits, grad_features, terms = slab_pass(scan_pixels[slab_index], labels[slab_index], conv1_weight, conv2_weight, context_weight, up_weight, skip_weight, class_weight)
        logit_list.append(logits)
        feature_list.append(grad_features)
        if totals is None:
            totals = terms
        else:
            totals = tuple((running + extra_term for running, extra_term in zip(totals, terms)))
    scaled = tuple((running / PIXELS for running in totals))
    return (jnp.stack(logit_list), jnp.stack(feature_list), scaled[0], scaled[1], scaled[2], scaled[3], scaled[4], scaled[5])
```

```python
import functools

import jax
import jax.numpy as jnp
from jax import lax
from jax.experimental import pallas as pl
from jax.experimental.pallas import tpu as pltpu
from jax.sharding import PartitionSpec as P

K = 8
COLUMN_SPREAD = 16
TAPS = 7
BOTH = ("tile", "dp")
VMEM = pl.BlockSpec(memory_space=pltpu.VMEM)
SMEM = pl.BlockSpec(memory_space=pltpu.SMEM)
ANY = pl.BlockSpec(memory_space=pl.ANY)


def params(mebibytes):
    return pltpu.CompilerParams(vmem_limit_bytes=mebibytes * 1024 * 1024)


def flip(value, tile_mask, dp_mask):
    tiles, slabs = lax.axis_size("tile"), lax.axis_size("dp")
    route = [
        (t * slabs + z, (t ^ tile_mask) * slabs + (z ^ dp_mask))
        for t in range(tiles)
        for z in range(slabs)
    ]
    return lax.ppermute(value, BOTH, route)


def bits(count):
    return count.bit_length() - 1


def position():
    t, z = lax.axis_index("tile"), lax.axis_index("dp")
    return t, z, (z & 1) ^ ((z >> 1) & 1)


def row_pairs(rows):
    out = []
    for first in range(0, rows, 2):
        pair = [i for i in (first, first + 1) if i < rows]
        low = max(0, pair[0] - 3)
        high = min(rows, pair[-1] + 4)
        out.append((pair, low, high))
    return out


def wgrad_kernel(chips, rows, width, block, place, *refs):
    masks = 2 * chips
    own, other = refs[0], refs[1]
    grads = refs[2 : 2 + masks]
    out, features, wide, stacked, total = refs[2 + masks :]
    chip, core = place[0] >> 1, place[0] & 1
    columns = 2 * chips * width
    for m in range(masks):
        slab, mask = m // chips, m % chips
        for k in range(2):
            tile = 2 * (chip ^ mask) + (core ^ k)
            at = pl.multiple_of(tile * width, width)
            for i in range(rows):
                features[slab, i, pl.ds(at, width), :] = (own, other)[k][m, i]
                wide[slab, i, :, pl.ds(pl.multiple_of(at + 128, 128), width)] = grads[m][
                    k, :, i * width : (i + 1) * width
                ].astype(jnp.float32)
    for slab in range(2):
        for i in range(rows):
            edge = jnp.zeros((block, 128), jnp.float32)
            wide[slab, i, :, 0:128] = edge
            wide[slab, i, :, 128 + columns : 256 + columns] = edge
            for b in range(TAPS):
                start = 128 - (b - 3) * COLUMN_SPREAD
                stacked[slab, i, b * block : (b + 1) * block, :] = wide[
                    slab, i, :, start : start + columns
                ].astype(jnp.bfloat16)
    total[...] = jnp.zeros_like(total)
    for slab in range(2):
        for pair, low, high in row_pairs(rows):
            lhs = stacked[slab, low:high].reshape((high - low) * TAPS * block, columns)
            rhs = jnp.concatenate([features[slab, i] for i in pair], axis=-1)
            result = jnp.dot(lhs, rhs, preferred_element_type=jnp.float32)
            for n, i in enumerate(pair):
                for j in range(low, high):
                    a = i - j + 3
                    if 0 <= a < TAPS:
                        total[a] += result[
                            (j - low) * TAPS * block : (j - low + 1) * TAPS * block,
                            n * 128 : (n + 1) * 128,
                        ]
    out[...] = total[...].reshape(out.shape).astype(jnp.bfloat16)


def wgrad(place, own, other, grads, chips, block):
    rows, width = own.shape[1], own.shape[2]
    columns = 2 * chips * width
    return pl.pallas_call(
        functools.partial(wgrad_kernel, chips, rows, width, block),
        out_shape=jax.ShapeDtypeStruct((TAPS * TAPS * block, 128), jnp.bfloat16),
        in_specs=[SMEM] + [VMEM] * (2 + len(grads)),
        out_specs=VMEM,
        scratch_shapes=[
            pltpu.VMEM((2, rows, columns, 128), jnp.bfloat16),
            pltpu.VMEM((2, rows, block, columns + 256), jnp.float32),
            pltpu.VMEM((2, rows, TAPS * block, columns), jnp.bfloat16),
            pltpu.VMEM((TAPS, TAPS * block, 128), jnp.float32),
        ],
        compiler_params=params(56),
        cost_estimate=pl.CostEstimate(
            flops=2 * 23 * 2 * TAPS * block * columns * 128,
            bytes_accessed=8_000_000,
            transcendentals=0,
        ),
        name="context_term",
    )(place, own, other, *grads)


def unpack_kernel(order, chips, block, first, groups, scale, place, *refs):
    sources, out, gathered, ready, sems = refs[:4], refs[-4], refs[-3], refs[-2], refs[-1]
    tile, half = place[0], place[1]
    chip, core = tile >> 1, tile & 1
    entries = sources[0].shape[0]

    def copy(slot, g):
        return pltpu.make_async_copy(ready.at[slot], out.at[first + g], sems.at[slot])

    def step(g, carry):
        slot = lax.rem(g, 2)
        at = pl.multiple_of(g * block, block)
        for n in range(4):
            for i in range(entries):
                index = i + entries * (n % 2)
                mask = sum(1 << d for q, d in enumerate(order) if (index >> q) & 1)
                whose = 2 * (chip ^ (mask % chips)) + (core ^ (n // 2))
                gathered[
                    half ^ (mask // chips), pl.ds(pl.multiple_of(whose * block, block), block), :
                ] = sources[n][i, pl.ds(at, block), :].astype(jnp.float32)

        @pl.when(g >= 2)
        def _():
            copy(slot, g - 2).wait()

        for u in range(2):
            ready[slot, u * 128 : (u + 1) * 128, :] = gathered[u].T * scale
        copy(slot, g).start()
        return carry

    lax.fori_loop(0, groups, step, 0)
    for g in range(max(0, groups - 2), groups):
        copy(g % 2, g).wait()


def unpack(place, sources, target, order, chips, block, first, groups, scale):
    wide = 2 * chips * block
    shape = jax.ShapeDtypeStruct((TAPS * TAPS, 256, wide), jnp.float32)
    operands = [place, *sources] + ([] if target is None else [target])
    return pl.pallas_call(
        functools.partial(unpack_kernel, order, chips, block, first, groups, scale),
        out_shape=shape,
        in_specs=[SMEM] + [VMEM] * 4 + ([] if target is None else [ANY]),
        out_specs=ANY,
        input_output_aliases={} if target is None else {5: 0},
        scratch_shapes=[
            pltpu.VMEM((2, wide, 128), jnp.float32),
            pltpu.VMEM((2, 256, wide), jnp.float32),
            pltpu.SemaphoreType.DMA((2,)),
        ],
        compiler_params=params(32),
        cost_estimate=pl.CostEstimate(
            flops=0, bytes_accessed=groups * 256 * wide * 6, transcendentals=0
        ),
        name="context_out",
    )(*operands)


def send_features(features):
    chips = lax.axis_size("tile") // 2
    _, _, half = position()
    halves = jnp.moveaxis(features.reshape(*features.shape[:2], 2, 128), 2, 0)
    mine = lax.dynamic_index_in_dim(halves, half, 0, False)
    theirs = lax.dynamic_index_in_dim(halves, 1 - half, 0, False)
    parts = []
    for m in range(2 * chips):
        block = theirs if m // chips else mine
        parts.append(block if m == 0 else flip(block, 2 * (m % chips), m // chips))
    own = jnp.stack(parts)
    return own, flip(own, 1, 0)


def send_gradient(gradient):
    tiles = lax.axis_size("tile")
    chips = tiles // 2
    t, _, _ = position()
    chip, core = t >> 1, t & 1
    pixels = gradient.shape[0] * gradient.shape[1]
    block = gradient.shape[2] // tiles
    turned = gradient.reshape(pixels, -1).T.reshape(chips, 2, block, pixels)
    mine = lax.dynamic_index_in_dim(turned, core, 1, False)
    theirs = lax.dynamic_index_in_dim(turned, 1 - core, 1, False)
    both = jnp.stack([mine, flip(theirs, 1, 0)], axis=1)
    parts = []
    for m in range(2 * chips):
        part = lax.dynamic_index_in_dim(both, chip ^ (m % chips), 0, False)
        parts.append(part if m == 0 else flip(part, 2 * (m % chips), m // chips))
    return parts, block


def fold_small(small, chips):
    t, _, half = position()
    packed = jnp.concatenate([term.reshape(-1, 128) for term in small])
    unit = 16 * 4 * chips
    short = -packed.shape[0] % unit
    packed = jnp.concatenate([packed, jnp.zeros((short, 128), jnp.float32)])
    steps = [(1, 0, t & 1)]
    for d in range(bits(chips)):
        steps.append((2 << d, 0, (t >> (d + 1)) & 1))
    steps.append((0, 1, half))
    for tile_mask, dp_mask, bit in steps:
        pairs = packed.reshape(-1, 2, packed.shape[0] // 2, 128)[0]
        mine = lax.dynamic_index_in_dim(pairs, bit, 0, False)
        theirs = lax.dynamic_index_in_dim(pairs, 1 - bit, 0, False).astype(jnp.bfloat16)
        packed = mine + flip(theirs, tile_mask, dp_mask).astype(jnp.float32)
    return packed.astype(jnp.bfloat16)


def unfold_small(place, sources, order, chips, scale):
    acc, last, near, far = sources
    dims = len(order)
    own = jnp.concatenate([acc, last])
    sibling = jnp.concatenate([near, far])
    cube = jnp.stack([own, sibling]).reshape([2] * (dims + 1) + list(own.shape[1:]))
    names = ["core"] + [order[q] for q in reversed(range(dims))]
    wanted = ["core", *range(dims)]
    cube = jnp.transpose(
        cube, [names.index(n) for n in wanted] + [dims + 1, dims + 2]
    ).astype(jnp.float32)
    tile, half = place[0], place[1]
    flags = [tile & 1] + [(tile >> (d + 1)) & 1 for d in range(dims - 1)] + [half]
    for axis, flag in enumerate(flags):
        cube = jnp.where(flag == 1, jnp.flip(cube, axis), cube)
    return cube.reshape(-1, 128) * scale


def sum_and_share(term, small, place, chips, block, scale):
    dims = bits(chips) + 1
    groups = TAPS * TAPS
    bounds = [groups * p // dims for p in range(dims + 1)]
    parts = []
    for p in range(dims):
        part = term[bounds[p] * block : bounds[p + 1] * block]
        if p == dims - 1:
            part = jnp.concatenate([part, small])
        mask = 3
        while mask < lax.axis_size("dp"):
            other = flip(part, 0, mask)
            part = (part.astype(jnp.float32) + other.astype(jnp.float32)).astype(jnp.bfloat16)
            mask = 4 if mask == 3 else 2 * mask
        parts.append(part[None])
    orders = [[(p + q) % dims for q in range(dims)] for p in range(dims)]

    def across(value, dim):
        return flip(value, 2 << dim, 0) if dim < dims - 1 else flip(value, 0, 1)

    for q in range(dims - 1):
        parts = [
            jnp.concatenate([part, across(part, orders[p][q])]) for p, part in enumerate(parts)
        ]
    last = [across(part, orders[p][-1]) for p, part in enumerate(parts)]
    near = [flip(part, 1, 0) for part in parts]
    far = [flip(part, 1, 0) for part in last]
    target = None
    for p in range(dims):
        sources = (parts[p], last[p], near[p], far[p])
        target = unpack(
            place,
            sources,
            target,
            orders[p],
            chips,
            block,
            bounds[p],
            bounds[p + 1] - bounds[p],
            scale,
        )
    at = (groups - bounds[-2]) * block
    tails = [value[:, at:] for value in sources]
    return target, unfold_small(place, tails, orders[-1], chips, scale)


def shifted(block, axis, distance):
    devices = range(lax.axis_size(axis))
    route = [(i - distance, i) for i in devices if i - distance in devices]
    return lax.ppermute(block, axis, route)


def padded(value, sides, width):
    for axis, dim in sides:
        peers, length = (lax.axis_size(axis), value.shape[dim])
        up = [(i, (i + 1) % peers) for i in range(peers - 1)]
        down = [(j, i) for i, j in up]
        last = lax.slice_in_dim(value, length - width, length, axis=dim)
        initial = lax.slice_in_dim(value, 0, width, axis=dim)
        before = lax.ppermute(last, axis, up)
        after = lax.ppermute(initial, axis, down)
        value = jnp.concatenate([before, value, after], axis=dim)
    return value


def product(pattern, lhs_array, rhs_array):
    return jnp.einsum(pattern, lhs_array, rhs_array, preferred_element_type=jnp.float32)


def silu_slope(inputs):
    sigmoid_value = jax.nn.sigmoid(inputs)
    return sigmoid_value + inputs * sigmoid_value * (1.0 - sigmoid_value)


def column_taps(feature_map, left_edge):
    channels = feature_map.shape[-1] // 2
    even_cols = feature_map[..., :channels]
    odd_cols = feature_map[..., channels:]
    before_cols = jnp.concatenate([left_edge, odd_cols[:, :-1]], axis=1)
    joined = jnp.concatenate([before_cols, even_cols, odd_cols], axis=-1)
    paired = joined.reshape(joined.shape[0] // 2, 2, joined.shape[1], joined.shape[2])
    row_even = paired[:, 0]
    row_odd = paired[:, 1]
    row_before = jnp.concatenate([jnp.zeros_like(row_odd[:1]), row_odd[:-1]], axis=0)
    return (row_before, row_even, row_odd)


def conv_apply(taps, weight):
    running = product("rwc,cd->rwd", taps[0], weight[0])
    for tap_index in range(1, 3):
        running = running + product("rwc,cd->rwd", taps[tap_index], weight[tap_index])
    return running


def conv_weight_grad(taps, gradient):
    return jnp.stack([product("rwc,rwd->cd", taps[tap_index], gradient) for tap_index in range(3)])


def taps_back(gradient, weight, channels):
    grad_taps = [product("rwd,cd->rwc", gradient, weight[tap_index]) for tap_index in range(3)]
    grad_before, grad_even, grad_odd = grad_taps
    grad_odd = grad_odd + jnp.concatenate(
        [grad_before[1:], jnp.zeros_like(grad_before[:1])], axis=0
    )
    joined = jnp.stack([grad_even, grad_odd], axis=1)
    joined = joined.reshape(2 * grad_even.shape[0], grad_even.shape[1], grad_even.shape[2])
    col_before = joined[..., :channels]
    col_even = joined[..., channels : 2 * channels]
    col_odd = joined[..., 2 * channels :]
    col_odd = col_odd + jnp.concatenate(
        [col_before[:, 1:], jnp.zeros_like(col_before[:, :1])], axis=1
    )
    return (jnp.concatenate([col_even, col_odd], axis=-1), col_before[:, :1])


def context_taps(widened_map, slab_height, slab_width):
    bordered_map = jnp.pad(widened_map, ((3, 3), (0, 0), (0, 0)))
    return [
        jnp.concatenate(
            [
                bordered_map[
                    row_offset : row_offset + slab_height,
                    column_offset * COLUMN_SPREAD : column_offset * COLUMN_SPREAD + slab_width,
                ]
                for column_offset in range(7)
            ],
            axis=-1,
        )
        for row_offset in range(7)
    ]


def context_apply(stacks, weight):
    running = product("rwc,cd->rwd", stacks[0], weight[0])
    for row_offset in range(1, 7):
        running = running + product("rwc,cd->rwd", stacks[row_offset], weight[row_offset])
    return running


def context_back(widened_gradient, weight, slab_height, slab_width, channels):
    bordered_map = jnp.pad(widened_gradient, ((3, 3), (0, 0), (0, 0)))
    running = jnp.zeros((slab_height, slab_width, channels), jnp.float32)
    for row_offset in range(7):
        leading_row = 6 - row_offset
        picked_values = jnp.concatenate(
            [
                bordered_map[
                    leading_row : leading_row + slab_height,
                    (6 - column_offset) * COLUMN_SPREAD : (6 - column_offset) * COLUMN_SPREAD
                    + slab_width,
                ]
                for column_offset in range(7)
            ],
            axis=-1,
        )
        picked_values = picked_values.reshape(slab_height, slab_width, 7, channels)
        running = running + product(
            "rwbd,bcd->rwc", picked_values, weight[row_offset].reshape(7, channels, channels)
        )
    return running


def body(
    scan_pixels,
    labels,
    conv1_weight,
    conv2_weight,
    context_weight,
    up_weight,
    skip_weight,
    class_weight,
):
    image_tile = scan_pixels[0]
    label_tile = labels[0]
    channels_in = image_tile.shape[-1] // 2
    first_edge = shifted(image_tile[:, -1:, channels_in:], "tile", 1)
    first_taps = column_taps(image_tile, first_edge)
    first_pre = conv_apply(first_taps, conv1_weight)
    first_map = jax.nn.silu(first_pre).astype(jnp.bfloat16)
    half_rows, first_cols, width_one = first_map.shape
    second_field = first_map.reshape(half_rows, first_cols // 2, 2 * width_one)
    second_edge = shifted(second_field[:, -1:, width_one:], "tile", 1)
    second_taps = column_taps(second_field, second_edge)
    second_pre = conv_apply(second_taps, conv2_weight)
    later_feature_map = jax.nn.silu(second_pre).astype(jnp.bfloat16)
    slab_height, slab_width, width_two = later_feature_map.shape
    own_half, other_half = send_features(later_feature_map)
    widened_map = padded(later_feature_map, (("tile", 1),), 3 * COLUMN_SPREAD)
    stacks = context_taps(widened_map, slab_height, slab_width)
    context_pre = context_apply(stacks, context_weight)
    context = (later_feature_map.astype(jnp.float32) + jax.nn.silu(context_pre)).astype(
        jnp.bfloat16
    )
    coarse_mix = product("rwc,cd->rwd", context, up_weight)
    upsampled = jnp.broadcast_to(
        coarse_mix[:, None, :, None, :], (slab_height, 2, slab_width, 2, width_one)
    ).reshape(half_rows, first_cols, width_one)
    decoder_pre = product("rwc,cd->rwd", first_map, skip_weight) + upsampled
    decoded = jax.nn.silu(decoder_pre).astype(jnp.bfloat16)
    logits = product("rwc,kc->krw", decoded, class_weight)
    target = (label_tile[None] == jnp.arange(K, dtype=jnp.int32)[:, None, None]).astype(jnp.float32)
    grad_logits = (jax.nn.sigmoid(logits) - target).astype(jnp.bfloat16)
    out_term = product("krw,rwc->kc", grad_logits, decoded)
    grad_decoded = product("krw,kc->rwc", grad_logits, class_weight)
    grad_decoder = (grad_decoded * silu_slope(decoder_pre)).astype(jnp.bfloat16)
    skip_term = product("rwc,rwd->cd", first_map, grad_decoder)
    pooled = (
        grad_decoder.astype(jnp.float32)
        .reshape(slab_height, 2, slab_width, 2, width_one)
        .sum(axis=(1, 3))
        .astype(jnp.bfloat16)
    )
    up_term = product("rwc,rwd->cd", context, pooled)
    grad_context_map = product("rwd,cd->rwc", pooled, up_weight)
    skip_features = product("rwd,cd->rwc", grad_decoder, skip_weight)
    context_input_gradient = (grad_context_map * silu_slope(context_pre)).astype(jnp.bfloat16)
    parts, block = send_gradient(context_input_gradient)
    widened_gradient = padded(context_input_gradient, (("tile", 1),), 3 * COLUMN_SPREAD)
    grad_second = grad_context_map + context_back(
        widened_gradient, context_weight, slab_height, slab_width, width_two
    )
    second_grad = (grad_second * silu_slope(second_pre)).astype(jnp.bfloat16)
    conv2_term = conv_weight_grad(second_taps, second_grad)
    grad_field, grad_edge = taps_back(second_grad, conv2_weight, width_one)
    returned = shifted(grad_edge, "tile", -1)
    last_pair = grad_field[:, -1:] + jnp.concatenate([jnp.zeros_like(returned), returned], axis=-1)
    grad_field = jnp.concatenate([grad_field[:, :-1], last_pair], axis=1)
    grad_features = skip_features + grad_field.reshape(half_rows, first_cols, width_one)
    first_grad = (grad_features * silu_slope(first_pre)).astype(jnp.bfloat16)
    conv1_term = conv_weight_grad(first_taps, first_grad)
    tiles = lax.axis_size("tile")
    pixel_count = lax.axis_size("dp") * half_rows * first_cols * tiles
    scale = 1.0 / pixel_count
    t, _, half = position()
    place = jnp.stack([t, half]).astype(jnp.int32)
    context_term = wgrad(place, own_half, other_half, parts, tiles // 2, block)
    small = [conv1_term, conv2_term, up_term, skip_term, out_term]
    folded = fold_small(small, tiles // 2)
    grad_context, packed = sum_and_share(context_term, folded, place, tiles // 2, block, scale)
    scaled, at = [], 0
    for term in small:
        count = term.size // 128
        scaled.append(packed[at : at + count].reshape(term.shape))
        at += count
    return (
        logits[None],
        grad_features[None],
        scaled[0],
        scaled[1],
        grad_context.reshape(context_weight.shape),
        scaled[2],
        scaled[3],
        scaled[4],
    )


def solution(mesh):
    in_specs = (P("dp", None, "tile", None), P("dp", None, "tile"), P(), P(), P(), P(), P(), P())
    out_specs = (
        P("dp", None, None, "tile"),
        P("dp", None, "tile", None),
        P(),
        P(),
        P(),
        P(),
        P(),
        P(),
    )
    return jax.shard_map(body, mesh=mesh, in_specs=in_specs, out_specs=out_specs, check_vma=False)
```

```python
import functools

import jax
import jax.numpy as jnp
from jax import lax
from jax.experimental import pallas as pl
from jax.experimental.pallas import tpu as pltpu
from jax.sharding import PartitionSpec as P

K = 8
COLUMN_SPREAD = 16
TAPS = 7
BOTH = ("tile", "dp")
VMEM = pl.BlockSpec(memory_space=pltpu.VMEM)
SMEM = pl.BlockSpec(memory_space=pltpu.SMEM)
ANY = pl.BlockSpec(memory_space=pl.ANY)

LIGHT = pl.CostEstimate(flops=1000, bytes_accessed=1000, transcendentals=0)


def params(mebibytes):
    return pltpu.CompilerParams(vmem_limit_bytes=mebibytes * 1024 * 1024)


def flip(value, tile_mask, dp_mask):
    tiles, slabs = lax.axis_size("tile"), lax.axis_size("dp")
    route = [
        (t * slabs + z, (t ^ tile_mask) * slabs + (z ^ dp_mask))
        for t in range(tiles)
        for z in range(slabs)
    ]
    return lax.ppermute(value, BOTH, route)


def bits(count):
    return count.bit_length() - 1


def position():
    t, z = lax.axis_index("tile"), lax.axis_index("dp")
    return t, z, (z & 1) ^ ((z >> 1) & 1)


def row_pairs(rows):
    out = []
    for first in range(0, rows, 2):
        pair = [i for i in (first, first + 1) if i < rows]
        low = max(0, pair[0] - 3)
        high = min(rows, pair[-1] + 4)
        out.append((pair, low, high))
    return out


def wgrad_kernel(chips, rows, width, block, place, *refs):
    masks = 2 * chips
    own, other = refs[:masks], refs[masks : 2 * masks]
    out, features, wide, stacked, total = refs[2 * masks :]
    chip, core = place[0] >> 1, place[0] & 1
    columns = 2 * chips * width
    for m in range(masks):
        slab, mask = m // chips, m % chips
        for k in range(2):
            tile = 2 * (chip ^ mask) + (core ^ k)
            at = pl.multiple_of(tile * width, width)
            for i in range(rows):
                start = (rows * (width + k * block)) + i * block
                features[slab, i, pl.ds(at, width), :] = (own, other)[k][m][
                    i * width : (i + 1) * width, :
                ]
                wide[slab, i, :, pl.ds(pl.multiple_of(at + 128, 128), width)] = own[m][
                    start : start + block, :
                ].astype(jnp.float32)
    for slab in range(2):
        for i in range(rows):
            edge = jnp.zeros((block, 128), jnp.float32)
            wide[slab, i, :, 0:128] = edge
            wide[slab, i, :, 128 + columns : 256 + columns] = edge
            for b in range(TAPS):
                start = 128 - (b - 3) * COLUMN_SPREAD
                stacked[slab, i, b * block : (b + 1) * block, :] = wide[
                    slab, i, :, start : start + columns
                ].astype(jnp.bfloat16)
    total[...] = jnp.zeros_like(total)
    for slab in range(2):
        for pair, low, high in row_pairs(rows):
            lhs = stacked[slab, low:high].reshape((high - low) * TAPS * block, columns)
            rhs = jnp.concatenate([features[slab, i] for i in pair], axis=-1)
            result = jnp.dot(lhs, rhs, preferred_element_type=jnp.float32)
            for n, i in enumerate(pair):
                for j in range(low, high):
                    a = i - j + 3
                    if 0 <= a < TAPS:
                        total[a] += result[
                            (j - low) * TAPS * block : (j - low + 1) * TAPS * block,
                            n * 128 : (n + 1) * 128,
                        ]
    out[...] = total[...].reshape(out.shape).astype(jnp.bfloat16)


def wgrad(place, own, other, chips, rows, width, block):
    columns = 2 * chips * width
    return pl.pallas_call(
        functools.partial(wgrad_kernel, chips, rows, width, block),
        out_shape=jax.ShapeDtypeStruct((TAPS * TAPS * block, 128), jnp.bfloat16),
        in_specs=[SMEM] + [VMEM] * (2 * len(own)),
        out_specs=VMEM,
        scratch_shapes=[
            pltpu.VMEM((2, rows, columns, 128), jnp.bfloat16),
            pltpu.VMEM((2, rows, block, columns + 256), jnp.float32),
            pltpu.VMEM((2, rows, TAPS * block, columns), jnp.bfloat16),
            pltpu.VMEM((TAPS, TAPS * block, 128), jnp.float32),
        ],
        compiler_params=params(56),
        cost_estimate=LIGHT,
        name="context_term",
    )(place, *own, *other)


def pack_kernel(chips, rows, width, block, place, features, mine, theirs, *messages):
    half = place[1]
    for m, message in enumerate(messages):
        mask = m % chips
        at = pl.multiple_of((half ^ (m // chips)) * 128, 128)
        for i in range(rows):
            message[i * width : (i + 1) * width, :] = features[i, :, pl.ds(at, 128)]
            for k, part in enumerate((mine, theirs)):
                start = rows * (width + k * block) + i * block
                message[start : start + block, :] = part[mask, i]


def pack(place, features, mine, theirs):
    rows, width = features.shape[0], features.shape[1]
    chips, block = mine.shape[0], mine.shape[2]
    shape = jax.ShapeDtypeStruct((rows * (width + 2 * block), 128), jnp.bfloat16)
    return pl.pallas_call(
        functools.partial(pack_kernel, chips, rows, width, block),
        out_shape=[shape] * (2 * chips),
        in_specs=[SMEM] + [VMEM] * 3,
        out_specs=[VMEM] * (2 * chips),
        compiler_params=params(56),
        cost_estimate=LIGHT,
        name="pack",
    )(place, features, mine, theirs)


def unpack_kernel(orders, bounds, chips, block, place, *refs):
    parts = len(orders)
    sources = [refs[4 * p : 4 * p + 4] for p in range(parts)]
    out = refs[4 * parts]
    gathered, ready, sems = refs[4 * parts + 1 :]
    tile, half = place[0], place[1]
    chip, core = tile >> 1, tile & 1
    ones = [lax.broadcasted_iota(jnp.int32, (128, 128), n) for n in range(2)]
    identity = (ones[0] == ones[1]).astype(jnp.bfloat16)
    batches = [
        (p, n, min(4, bounds[p + 1] - n))
        for p in range(parts)
        for n in range(bounds[p], bounds[p + 1], 4)
    ]

    def copy(n):
        _, start, count = batches[n]
        return pltpu.make_async_copy(
            ready.at[n % 2, 0:count], out.at[start : start + count], sems.at[n % 2]
        )

    for n, (p, start, count) in enumerate(batches):
        entries = sources[p][0].shape[0]
        for s in range(4):
            for i in range(entries):
                index = i + entries * (s % 2)
                mask = sum(1 << d for q, d in enumerate(orders[p]) if (index >> q) & 1)
                whose = 2 * (chip ^ (mask % chips)) + (core ^ (s // 2))
                for g in range(count):
                    at = (start - bounds[p] + g) * block
                    gathered[
                        n % 2,
                        g,
                        half ^ (mask // chips),
                        pl.ds(pl.multiple_of(whose * block, block), block),
                        :,
                    ] = sources[p][s][i, at : at + block, :]
        if n >= 2:
            copy(n - 2).wait()
        for g in range(count):
            for u in range(2):
                ready[n % 2, g, u * 128 : (u + 1) * 128, :] = dot(
                    identity, gathered[n % 2, g, u], NT
                )
        copy(n).start()
    for n in range(max(0, len(batches) - 2), len(batches)):
        copy(n).wait()


def unpack(place, sources, orders, bounds, chips, block):
    wide = 2 * chips * block
    operands = [array for group in sources for array in group]
    return pl.pallas_call(
        functools.partial(unpack_kernel, orders, bounds, chips, block),
        out_shape=jax.ShapeDtypeStruct((TAPS * TAPS, 256, wide), jnp.float32),
        in_specs=[SMEM] + [VMEM] * len(operands),
        out_specs=ANY,
        scratch_shapes=[
            pltpu.VMEM((2, 4, 2, wide, 128), jnp.bfloat16),
            pltpu.VMEM((2, 4, 256, wide), jnp.float32),
            pltpu.SemaphoreType.DMA((2,)),
        ],
        compiler_params=params(56),
        cost_estimate=LIGHT,
        name="context_out",
    )(place, *operands)


def fold_small(packed, chips, first):
    t, _, half = position()
    steps = [(1, 0, t & 1)]
    for d in range(bits(chips)):
        steps.append((2 << d, 0, (t >> (d + 1)) & 1))
    steps.append((0, 1, half))
    for tile_mask, dp_mask, bit in steps:
        pairs = packed.reshape(2, packed.shape[0] // 2, 128)
        mine = lax.dynamic_index_in_dim(pairs, bit, 0, False)
        theirs = lax.dynamic_index_in_dim(pairs, 1 - bit, 0, False).astype(jnp.bfloat16)
        packed = mine + flip(theirs, tile_mask, dp_mask).astype(jnp.float32)
        if tile_mask == 1:
            packed, first = lax.optimization_barrier((packed, first))
    return packed.astype(jnp.bfloat16), first


def sum_and_share(term, small, place, chips, block, scale, results, packed_rows):
    dims = bits(chips) + 1
    groups = TAPS * TAPS
    bounds = [groups * p // dims for p in range(dims + 1)]
    parts = [term[bounds[p] * block : bounds[p + 1] * block] for p in range(dims)]
    parts.append(small)
    totals, mask = [part.astype(jnp.float32) for part in parts], 3
    while mask < lax.axis_size("dp"):
        parts = [total.astype(jnp.bfloat16) for total in totals]
        others = [flip(part, 0, mask) for part in parts]
        others, results = lax.optimization_barrier((others, results))
        totals = [
            part.astype(jnp.float32) + other.astype(jnp.float32)
            for part, other in zip(parts, others)
        ]
        mask = 4 if mask == 3 else 2 * mask
    totals[-2:] = [jnp.concatenate(totals[-2:])]
    parts = [(total * scale).astype(jnp.bfloat16)[None] for total in totals]
    orders = [[(p + q) % dims for q in range(dims)] for p in range(dims)]

    def across(value, dim):
        return flip(value, 2 << dim, 0) if dim < dims - 1 else flip(value, 0, 1)

    for q in range(dims - 1):
        others = [across(part, orders[p][q]) for p, part in enumerate(parts)]
        others = lax.optimization_barrier(others)
        parts = [jnp.concatenate(pair) for pair in zip(parts, others)]
    last = [across(part, orders[p][-1]) for p, part in enumerate(parts)]
    near = [flip(part, 1, 0) for part in parts]
    far = [flip(part, 1, 0) for part in last]
    sources = list(zip(parts, last, near, far))
    target = unpack(place, sources, orders, bounds, chips, block)
    sources = sources[-1]
    return target, unpack_small(place, sources, orders[-1], chips, packed_rows), results


def dot(lhs, rhs, dims=((1,), (0,))):
    return lax.dot_general(lhs, rhs, (dims, ((), ())), preferred_element_type=jnp.float32)


NT = ((1,), (1,))
TN = ((0,), (0,))


def encode_kernel(image, halo, weight1, weight2, taps, slope1, features, slope2, odd):
    rows, pairs = image.shape[0] // 2, image.shape[1]
    empty = jnp.zeros((pairs + 16, 256), jnp.bfloat16)

    def line(n):
        if n < 0:
            return empty
        return jnp.concatenate([halo[n], image[n]], axis=0)

    lhs = jnp.concatenate(
        [
            jnp.concatenate([line(2 * i + a - 1) for i in range(rows)], axis=0)
            for a in range(3)
        ],
        axis=1,
    )
    none = jnp.zeros((64, 128), jnp.bfloat16)
    rhs = []
    for a in range(3):
        for_odd = jnp.concatenate([none, weight1[a]], axis=0)
        for_even = jnp.concatenate([weight1[a, 64:], none, none], axis=0)
        for_next = jnp.concatenate([none, none, none, weight1[a, :64]], axis=0)
        rhs.append(jnp.concatenate([for_odd, for_even, for_next], axis=1))
    result = dot(lhs, jnp.concatenate(rhs, axis=0)).reshape(rows, pairs + 16, 384)
    odd[...] = result[:, :, 256:384]
    even_pre = result[:, 16:, 128:256] + odd[:, 15 : 15 + pairs, :]
    gate = jax.nn.sigmoid(even_pre)
    value = even_pre * gate
    taps[:, :, 128:256] = value.astype(jnp.bfloat16)
    slope1[:, :, 0:128] = gate + value * (1.0 - gate)
    odd_pre = result[:, :, 0:128]
    gate = jax.nn.sigmoid(odd_pre)
    value = odd_pre * gate
    odd[...] = value
    taps[:, :, 256:384] = value[:, 16:].astype(jnp.bfloat16)
    slope1[:, :, 128:256] = (gate + value * (1.0 - gate))[:, 16:]
    taps[:, :, 0:128] = odd[:, 15 : 15 + pairs, :].astype(jnp.bfloat16)
    empty = jnp.zeros((pairs, 384), jnp.bfloat16)
    lhs = jnp.concatenate(
        [
            jnp.concatenate(
                [
                    empty if 2 * i + a < 1 else taps[2 * i + a - 1]
                    for i in range(rows // 2)
                ],
                axis=0,
            )
            for a in range(3)
        ],
        axis=1,
    )
    pre = dot(lhs, weight2[...].reshape(1152, 256))
    gate = jax.nn.sigmoid(pre)
    value = pre * gate
    features[...] = value.astype(jnp.bfloat16).reshape(features.shape)
    slope2[...] = (gate + value * (1.0 - gate)).reshape(slope2.shape)


def encode(image, halo, weight1, weight2):
    rows, pairs = image.shape[0] // 2, image.shape[1]
    bf16, f32 = jnp.bfloat16, jnp.float32
    return pl.pallas_call(
        encode_kernel,
        out_shape=[
            jax.ShapeDtypeStruct((rows, pairs, 384), bf16),
            jax.ShapeDtypeStruct((rows, pairs, 256), f32),
            jax.ShapeDtypeStruct((rows // 2, pairs, 256), bf16),
            jax.ShapeDtypeStruct((rows // 2, pairs, 256), f32),
        ],
        in_specs=[VMEM] * 4,
        out_specs=[VMEM] * 4,
        scratch_shapes=[pltpu.VMEM((rows, pairs + 16, 128), f32)],
        compiler_params=params(56),
        cost_estimate=LIGHT,
        name="encode",
    )(image, halo, weight1, weight2)


def widen(wide, left, middle, right):
    width = middle.shape[1]
    wide[:, 0:48, :] = left[...]
    wide[:, 48 : 48 + width, :] = middle[...]
    wide[:, 48 + width : 96 + width, :] = right[...]


def decode_kernel(
    chips,
    block,
    place,
    left,
    features,
    right,
    weight,
    taps,
    labels,
    up,
    skip,
    classes,
    logits,
    gradient,
    mine,
    theirs,
    context,
    pooled,
    grad_decoder,
    out_term,
    wide,
    total,
    turned,
):
    rows, width = features.shape[0], features.shape[1]
    step = pl.program_id(0)

    @pl.when(step == 0)
    def _():
        widen(wide, left, features, right)
        total[...] = jnp.zeros_like(total)

    for a in range(TAPS):

        @pl.when(step == a)
        def _(a=a):
            low, high = max(0, 3 - a), min(rows, rows + 3 - a)
            lhs = jnp.concatenate(
                [
                    wide[
                        low + a - 3 : high + a - 3,
                        b * COLUMN_SPREAD : b * COLUMN_SPREAD + width,
                        :,
                    ].reshape((high - low) * width, 256)
                    for b in range(TAPS)
                ],
                axis=1,
            )
            total[low * width : high * width, :] += dot(lhs, weight[0])

    @pl.when(step == TAPS - 1)
    def _():
        pixels = rows * width
        pre = total[...]
        gate = jax.nn.sigmoid(pre)
        value = pre * gate
        total[...] = gate + value * (1.0 - gate)
        mixed = features[...].reshape(pixels, 256).astype(jnp.float32) + value
        mixed = mixed.astype(jnp.bfloat16)
        context[...] = mixed
        coarse = dot(mixed, up[...])
        pool = jnp.zeros((pixels, 128), jnp.float32)
        outer = jnp.zeros((K, 128), jnp.float32)
        kinds = lax.broadcasted_iota(jnp.int32, (K, pixels), 0).astype(jnp.float32)
        source, place_at = [lax.broadcasted_iota(jnp.int32, (256, 256), n) for n in range(2)]
        split = (source == 2 * (place_at & 127) + (place_at >> 7)).astype(jnp.bfloat16)
        parted = dot(labels[...].astype(jnp.float32).astype(jnp.bfloat16), split)
        for p in range(2):
            for q in range(2):
                fine = jnp.concatenate(
                    [taps[2 * i + q, :, 128 + 128 * p : 256 + 128 * p] for i in range(rows)],
                    axis=0,
                )
                pre = dot(fine, skip[...]) + coarse
                gate = jax.nn.sigmoid(pre)
                value = pre * gate
                decoded = value.astype(jnp.bfloat16)
                scores = dot(classes[...], decoded, NT)
                logits[p, q] = scores
                wanted = jnp.concatenate(
                    [
                        parted[2 * i + q : 2 * i + q + 1, p * 128 : (p + 1) * 128]
                        for i in range(rows)
                    ],
                    axis=1,
                )
                target = (kinds == wanted).astype(jnp.float32)
                grad = (jax.nn.sigmoid(scores) - target).astype(jnp.bfloat16)
                outer += dot(grad, decoded)
                back = dot(grad, classes[...], TN) * (gate + value * (1.0 - gate))
                back = back.astype(jnp.bfloat16)
                grad_decoder[p, q] = back
                pool += back.astype(jnp.float32)
        out_term[...] = outer
        small = pool.astype(jnp.bfloat16)
        pooled[...] = small
        result = dot(small, up[...], NT) * total[...]
        gradient[...] = result.astype(jnp.bfloat16).reshape(gradient.shape)
        for i in range(rows):
            line = result[i * width : (i + 1) * width].T.astype(jnp.bfloat16)
            turned[:, i] = line.reshape(2 * chips, block, width)
        chip, core = place[0] >> 1, place[0] & 1
        for mask in range(chips):
            mine[mask] = turned[2 * (chip ^ mask) + core]
            theirs[mask] = turned[2 * (chip ^ mask) + 1 - core]


def whole(shape):
    return pl.BlockSpec(shape, lambda n: (0,) * len(shape))


def decode(place, left, features, right, weight, taps, labels, up, skip, classes, chips):
    rows, width = features.shape[0], features.shape[1]
    pixels = rows * width
    block = 128 // chips
    bf16, f32 = jnp.bfloat16, jnp.float32
    operands = (left, features, right, weight, taps, labels, up, skip, classes)
    specs = [whole(x.shape) for x in operands]
    specs[3] = pl.BlockSpec((1, *weight.shape[1:]), lambda n: (n, 0, 0))
    outs = [
        jax.ShapeDtypeStruct((2, 2, K, pixels), f32),
        jax.ShapeDtypeStruct((rows, width, 256), bf16),
        jax.ShapeDtypeStruct((chips, rows, block, width), bf16),
        jax.ShapeDtypeStruct((chips, rows, block, width), bf16),
        jax.ShapeDtypeStruct((pixels, 256), bf16),
        jax.ShapeDtypeStruct((pixels, 128), bf16),
        jax.ShapeDtypeStruct((2, 2, pixels, 128), bf16),
        jax.ShapeDtypeStruct((K, 128), f32),
    ]
    return pl.pallas_call(
        functools.partial(decode_kernel, chips, block),
        out_shape=outs,
        grid=(TAPS,),
        in_specs=[SMEM, *specs],
        out_specs=[whole(x.shape) for x in outs],
        scratch_shapes=[
            pltpu.VMEM((rows, width + 96, 256), bf16),
            pltpu.VMEM((pixels, 256), f32),
            pltpu.VMEM((2 * chips, rows, block, width), bf16),
        ],
        compiler_params=params(56),
        cost_estimate=LIGHT,
        name="decode",
    )(place, *operands)


def back_kernel(
    left,
    gradient,
    right,
    weight,
    pooled,
    up,
    slope2,
    taps,
    grad_decoder,
    skip,
    weight2,
    context,
    partial,
    edge,
    term2,
    up_term,
    skip_term,
    wide,
    total,
    before,
):
    rows, width = gradient.shape[0], gradient.shape[1]
    pixels = rows * width
    step = pl.program_id(0)

    @pl.when(step == 0)
    def _():
        widen(wide, left, gradient, right)
        total[...] = dot(pooled[...], up[...], NT)

    for a in range(TAPS):

        @pl.when(step == a)
        def _(a=a):
            low, high = max(0, a - 3), min(rows, rows + a - 3)
            result = None
            for b in range(TAPS):
                at = (6 - b) * COLUMN_SPREAD
                lhs = wide[low - a + 3 : high - a + 3, at : at + width, :]
                lhs = lhs.reshape((high - low) * width, 256)
                one = dot(lhs, weight[0, b * 256 : (b + 1) * 256, :], NT)
                result = one if result is None else result + one
            total[low * width : high * width, :] += result

    @pl.when(step == TAPS - 1)
    def _():
        grad = (total[...] * slope2[...].reshape(pixels, 256)).astype(jnp.bfloat16)
        up_term[...] = dot(context[...], pooled[...], TN)
        backs = []
        for a in range(3):
            first = 1 if a == 0 else 0
            lhs = jnp.concatenate(
                [taps[2 * i + a - 1] for i in range(first, rows)], axis=0
            )
            term2[a] = dot(lhs, grad[first * width :], TN)
            backs.append(dot(grad, weight2[a], NT))
        skips = jnp.zeros((128, 128), jnp.float32)
        for p in range(2):
            for q in range(2):
                fine = jnp.concatenate(
                    [taps[2 * i + q, :, 128 + 128 * p : 256 + 128 * p] for i in range(rows)],
                    axis=0,
                )
                skips += dot(fine, grad_decoder[p, q], TN)
                through = dot(grad_decoder[p, q], skip[...], NT)
                for i in range(rows):
                    partial[2 * i + q, :, p * 128 : (p + 1) * 128] = through[
                        i * width : (i + 1) * width
                    ]
        skip_term[...] = skips
        before[:, width : width + 8, :] = jnp.zeros((2 * rows, 8, 128), jnp.float32)
        for i in range(rows):
            here = slice(i * width, (i + 1) * width)
            even = backs[1][here]
            odd = backs[2][here]
            if i + 1 < rows:
                odd = odd + backs[0][(i + 1) * width : (i + 2) * width]
            for q, line in enumerate((even, odd)):
                before[2 * i + q, 0:width, :] = line[:, 0:128]
                partial[2 * i + q, :, 0:128] += line[:, 128:256]
                partial[2 * i + q, :, 128:256] += (
                    line[:, 256:384] + before[2 * i + q, 1 : width + 1, :]
                )
        edge[...] = before[:, 0:1, :]


def back(left, gradient, right, weight, pooled, up, slope2, taps, grads, skip, weight2, context):
    rows, width = gradient.shape[0], gradient.shape[1]
    pixels = rows * width
    bf16, f32 = jnp.bfloat16, jnp.float32
    operands = (
        left, gradient, right, weight, pooled, up, slope2, taps, grads, skip, weight2, context,
    )
    specs = [whole(x.shape) for x in operands]
    specs[3] = pl.BlockSpec((1, *weight.shape[1:]), lambda n: (n, 0, 0))
    outs = [
        jax.ShapeDtypeStruct((2 * rows, width, 256), f32),
        jax.ShapeDtypeStruct((2 * rows, 1, 128), f32),
        jax.ShapeDtypeStruct((3, 384, 256), f32),
        jax.ShapeDtypeStruct((256, 128), f32),
        jax.ShapeDtypeStruct((128, 128), f32),
    ]
    return pl.pallas_call(
        back_kernel,
        out_shape=outs,
        grid=(TAPS,),
        in_specs=specs,
        out_specs=[whole(x.shape) for x in outs],
        scratch_shapes=[
            pltpu.VMEM((rows, width + 96, 256), bf16),
            pltpu.VMEM((pixels, 256), f32),
            pltpu.VMEM((2 * rows, width + 8, 128), f32),
        ],
        compiler_params=params(56),
        cost_estimate=LIGHT,
        name="back",
    )(*operands)


def finish_kernel(
    partial, returned, slope1, image, halo, term2, up_term, skip_term, out_term, out, packed, shifted_up
):
    rows, width = partial.shape[0], partial.shape[1]
    last = lax.broadcasted_iota(jnp.int32, (rows, width, 128), 1) == width - 1
    even = partial[:, :, 0:128]
    odd = partial[:, :, 128:256] + jnp.where(last, returned[...], 0.0)
    for i in range(rows):
        out[i, pl.ds(0, width, stride=2), :] = even[i]
        out[i, pl.ds(1, width, stride=2), :] = odd[i]
    even = even * slope1[:, :, 0:128]
    odd = (odd * slope1[:, :, 128:256]).astype(jnp.bfloat16)
    shifted_up[:, 0:16, :] = jnp.zeros((rows, 16, 128), jnp.float32)
    shifted_up[:, width + 8 : width + 16, :] = jnp.zeros((rows, 8, 128), jnp.float32)
    shifted_up[:, 15 : 15 + width, :] = even
    even = even.astype(jnp.bfloat16)
    moved = shifted_up[...].astype(jnp.bfloat16)
    rhs = jnp.concatenate([odd, even, moved[:, 16:]], axis=2)
    for a in range(3):
        first = 1 if a == 0 else 0
        lines = [2 * i + a - 1 for i in range(first, rows)]
        lhs = jnp.concatenate([image[n] for n in lines], axis=0)
        result = dot(lhs, rhs[first:].reshape((rows - first) * width, 384), TN)
        side = jnp.concatenate([halo[n] for n in lines], axis=0)
        outer = dot(side, moved[first:, 0:16].reshape((rows - first) * 16, 128), TN)
        at = 192 * a
        packed[at : at + 64, :] = (
            result[192:256, 256:384] + outer[192:256] + result[64:128, 0:128]
        )
        packed[at + 64 : at + 128, :] = result[0:64, 128:256] + result[128:192, 0:128]
        packed[at + 128 : at + 192, :] = result[64:128, 128:256] + result[192:256, 0:128]
        for n in range(2):
            at = 576 + 384 * (2 * a + n)
            packed[at : at + 384, :] = term2[a, :, n * 128 : (n + 1) * 128]
    packed[2880:3136, :] = up_term[...]
    packed[3136:3264, :] = skip_term[...]
    packed[3264:3272, :] = out_term[...]
    packed[3272:, :] = jnp.zeros((packed.shape[0] - 3272, 128), jnp.float32)


def finish(partial, returned, slope1, image, halo, terms, packed_rows):
    rows, width = partial.shape[0], partial.shape[1]
    f32 = jnp.float32
    return pl.pallas_call(
        finish_kernel,
        out_shape=[
            jax.ShapeDtypeStruct((rows, 2 * width, 128), f32),
            jax.ShapeDtypeStruct((packed_rows, 128), f32),
        ],
        in_specs=[VMEM] * 9,
        out_specs=[VMEM] * 2,
        scratch_shapes=[pltpu.VMEM((rows, width + 16, 128), f32)],
        compiler_params=params(56),
        cost_estimate=LIGHT,
        name="finish",
    )(partial, returned, slope1, image, halo, *terms)


def small_kernel(order, chips, place, *refs):
    sources, packed = refs[:4], refs[-1]
    conv1, conv2, up, skip, out = refs[4:-1]
    tile, half = place[0], place[1]
    chip, core = tile >> 1, tile & 1
    depth = packed.shape[0] // (4 * chips)
    dims = len(order)
    entries, height = sources[0].shape[0], sources[0].shape[1]
    for s in range(4):
        for i in range(entries):
            index = i + entries * (s % 2)
            mask = sum(1 << d for q, d in enumerate(order) if (index >> q) & 1)
            whose = chip ^ (mask % chips)
            at = core ^ (s // 2)
            for d in range(dims - 1):
                at = 2 * at + ((whose >> d) & 1)
            at = 2 * at + (half ^ (mask // chips))
            packed[pl.ds(pl.multiple_of(at * depth, depth), depth), :] = sources[s][
                i, height - depth :, :
            ].astype(jnp.float32)
    for a in range(3):
        conv1[a] = packed[192 * a : 192 * a + 192, :]
        for n in range(2):
            at = 576 + 384 * (2 * a + n)
            conv2[a, :, n * 128 : (n + 1) * 128] = packed[at : at + 384, :]
    up[...] = packed[2880:3136, :]
    skip[...] = packed[3136:3264, :]
    out[...] = packed[3264:3272, :]


def unpack_small(place, sources, order, chips, packed_rows):
    f32 = jnp.float32
    shapes = [(3, 192, 128), (3, 384, 256), (256, 128), (128, 128), (K, 128)]
    return pl.pallas_call(
        functools.partial(small_kernel, order, chips),
        out_shape=[jax.ShapeDtypeStruct(shape, f32) for shape in shapes],
        in_specs=[SMEM] + [VMEM] * 4,
        out_specs=[VMEM] * 5,
        scratch_shapes=[pltpu.VMEM((packed_rows, 128), f32)],
        compiler_params=params(56),
        cost_estimate=LIGHT,
        name="small_out",
    )(place, *sources)


def moved(block, distance):
    tiles = lax.axis_size("tile")
    route = [(i, i + distance) for i in range(tiles) if 0 <= i + distance < tiles]
    return lax.ppermute(block, "tile", route)


def edges(value):
    return moved(value[:, -48:], 1), moved(value[:, :48], -1)


def body(
    scan_pixels,
    labels,
    conv1_weight,
    conv2_weight,
    context_weight,
    up_weight,
    skip_weight,
    class_weight,
):
    bf16 = jnp.bfloat16
    tiles = lax.axis_size("tile")
    chips = tiles // 2
    t, _, half = position()
    place = jnp.stack([t, half]).astype(jnp.int32)
    lines, line_pairs, _ = scan_pixels[0].shape
    rows, width = lines // 4, line_pairs // 2
    corner = moved(scan_pixels[0, :, -2:, :].reshape(lines, 1, 256), 1)
    halo = jnp.concatenate([jnp.zeros((lines, 15, 256), bf16), corner], axis=1)
    image = scan_pixels[0].reshape(lines, width, 256)
    taps, slope1, features, slope2 = encode(image, halo, conv1_weight, conv2_weight)
    left, right = edges(features)
    logits, gradient, mine, theirs, context, pooled, grads, out_term = decode(
        place, left, features, right, context_weight, taps, labels[0],
        up_weight, skip_weight, class_weight, chips,
    )
    messages = pack(place, features, mine, flip(theirs, 1, 0))
    gradient, messages = lax.optimization_barrier((gradient, messages))
    own = [
        part if m == 0 else flip(part, 2 * (m % chips), m // chips)
        for m, part in enumerate(messages)
    ]
    left, right = edges(gradient)
    partial, edge, conv2_term, up_term, skip_term = back(
        left, gradient, right, context_weight, pooled, up_weight, slope2, taps, grads,
        skip_weight, conv2_weight, context,
    )
    returned = moved(edge, -1)
    partial, own = lax.optimization_barrier((partial, own))
    other = [flip(part, 1, 0) for part in own]
    packed_rows = -(-3272 // (64 * chips)) * 64 * chips
    grad_features, packed = finish(
        partial, returned, slope1, image, halo,
        (conv2_term, up_term, skip_term, out_term), packed_rows,
    )
    logits = logits.reshape(2, 2, K, rows, width).transpose(2, 3, 1, 4, 0)
    logits = logits.reshape(1, K, 2 * rows, 2 * width)
    grad_features = grad_features[None]
    scale = 1.0 / (lax.axis_size("dp") * tiles * 4 * rows * width)
    block = mine.shape[2]
    context_term = wgrad(place, own, other, chips, rows, width, block)
    folded, context_term = fold_small(packed, chips, context_term)
    grad_context, small, (logits, grad_features) = sum_and_share(
        context_term, folded, place, chips, block, scale, (logits, grad_features), packed_rows
    )
    return (
        logits,
        grad_features,
        small[0],
        small[1],
        grad_context.reshape(context_weight.shape),
        small[2],
        small[3],
        small[4],
    )


def solution(mesh):
    in_specs = (P("dp", None, "tile", None), P("dp", None, "tile"), P(), P(), P(), P(), P(), P())
    out_specs = (
        P("dp", None, None, "tile"),
        P("dp", None, "tile", None),
        P(),
        P(),
        P(),
        P(),
        P(),
        P(),
    )
    return jax.shard_map(body, mesh=mesh, in_specs=in_specs, out_specs=out_specs, check_vma=False)
```

```python
import functools

import jax
import jax.numpy as jnp
from jax import lax
from jax.experimental import pallas as pl
from jax.experimental.pallas import tpu as pltpu
from jax.sharding import PartitionSpec as P

K = 8
COLUMN_SPREAD = 16
TAPS = 7
BOTH = ("tile", "dp")
VMEM = pl.BlockSpec(memory_space=pltpu.VMEM)
SMEM = pl.BlockSpec(memory_space=pltpu.SMEM)
ANY = pl.BlockSpec(memory_space=pl.ANY)

LIGHT = pl.CostEstimate(flops=1000, bytes_accessed=1000, transcendentals=0)


def params(mebibytes):
    return pltpu.CompilerParams(vmem_limit_bytes=mebibytes * 1024 * 1024)


def flip(value, tile_mask, dp_mask):
    tiles, slabs = lax.axis_size("tile"), lax.axis_size("dp")
    route = [
        (t * slabs + z, (t ^ tile_mask) * slabs + (z ^ dp_mask))
        for t in range(tiles)
        for z in range(slabs)
    ]
    return lax.ppermute(value, BOTH, route)


def bits(count):
    return count.bit_length() - 1


def position():
    t, z = lax.axis_index("tile"), lax.axis_index("dp")
    return t, z, (z & 1) ^ ((z >> 1) & 1)


def row_pairs(rows):
    out = []
    for first in range(0, rows, 2):
        pair = [i for i in (first, first + 1) if i < rows]
        low = max(0, pair[0] - 3)
        high = min(rows, pair[-1] + 4)
        out.append((pair, low, high))
    return out


def wgrad_kernel(chips, rows, width, block, place, *refs):
    masks = 2 * chips
    own, other = refs[:masks], refs[masks : 2 * masks]
    out, features, wide, stacked, total = refs[2 * masks :]
    chip, core = place[0] >> 1, place[0] & 1
    columns = 2 * chips * width
    for m in range(masks):
        slab, mask = m // chips, m % chips
        for k in range(2):
            tile = 2 * (chip ^ mask) + (core ^ k)
            at = pl.multiple_of(tile * width, width)
            for i in range(rows):
                start = (rows * (width + k * block)) + i * block
                features[slab, i, pl.ds(at, width), :] = (own, other)[k][m][
                    i * width : (i + 1) * width, :
                ]
                wide[slab, i, :, pl.ds(pl.multiple_of(at + 128, 128), width)] = own[m][
                    start : start + block, :
                ].astype(jnp.float32)
    for slab in range(2):
        for i in range(rows):
            edge = jnp.zeros((block, 128), jnp.float32)
            wide[slab, i, :, 0:128] = edge
            wide[slab, i, :, 128 + columns : 256 + columns] = edge
            for b in range(TAPS):
                start = 128 - (b - 3) * COLUMN_SPREAD
                stacked[slab, i, b * block : (b + 1) * block, :] = wide[
                    slab, i, :, start : start + columns
                ].astype(jnp.bfloat16)
    total[...] = jnp.zeros_like(total)
    for slab in range(2):
        for pair, low, high in row_pairs(rows):
            lhs = stacked[slab, low:high].reshape((high - low) * TAPS * block, columns)
            rhs = jnp.concatenate([features[slab, i] for i in pair], axis=-1)
            result = jnp.dot(lhs, rhs, preferred_element_type=jnp.float32)
            for n, i in enumerate(pair):
                for j in range(low, high):
                    a = i - j + 3
                    if 0 <= a < TAPS:
                        total[a] += result[
                            (j - low) * TAPS * block : (j - low + 1) * TAPS * block,
                            n * 128 : (n + 1) * 128,
                        ]
    out[...] = total[...].reshape(out.shape).astype(jnp.bfloat16)


def wgrad(place, own, other, chips, rows, width, block):
    columns = 2 * chips * width
    return pl.pallas_call(
        functools.partial(wgrad_kernel, chips, rows, width, block),
        out_shape=jax.ShapeDtypeStruct((TAPS * TAPS * block, 128), jnp.bfloat16),
        in_specs=[SMEM] + [VMEM] * (2 * len(own)),
        out_specs=VMEM,
        scratch_shapes=[
            pltpu.VMEM((2, rows, columns, 128), jnp.bfloat16),
            pltpu.VMEM((2, rows, block, columns + 256), jnp.float32),
            pltpu.VMEM((2, rows, TAPS * block, columns), jnp.bfloat16),
            pltpu.VMEM((TAPS, TAPS * block, 128), jnp.float32),
        ],
        compiler_params=params(56),
        cost_estimate=LIGHT,
        name="context_term",
    )(place, *own, *other)


def pack_kernel(chips, rows, width, block, place, features, mine, theirs, *messages):
    half = place[1]
    for m, message in enumerate(messages):
        mask = m % chips
        at = pl.multiple_of((half ^ (m // chips)) * 128, 128)
        for i in range(rows):
            message[i * width : (i + 1) * width, :] = features[i, :, pl.ds(at, 128)]
            for k, part in enumerate((mine, theirs)):
                start = rows * (width + k * block) + i * block
                message[start : start + block, :] = part[mask, i]


def pack(place, features, mine, theirs):
    rows, width = features.shape[0], features.shape[1]
    chips, block = mine.shape[0], mine.shape[2]
    shape = jax.ShapeDtypeStruct((rows * (width + 2 * block), 128), jnp.bfloat16)
    return pl.pallas_call(
        functools.partial(pack_kernel, chips, rows, width, block),
        out_shape=[shape] * (2 * chips),
        in_specs=[SMEM] + [VMEM] * 3,
        out_specs=[VMEM] * (2 * chips),
        compiler_params=params(56),
        cost_estimate=LIGHT,
        name="pack",
    )(place, features, mine, theirs)


def write_small(chips, sources, packed, outs, chip, core, half):
    conv1, conv2, up, skip, out = outs
    depth = packed.shape[0] // (4 * chips)
    for s in range(2):
        for mask in range(2 * chips):
            whose = chip ^ (mask % chips)
            at = core ^ s
            for d in range(bits(chips)):
                at = 2 * at + ((whose >> d) & 1)
            at = 2 * at + (half ^ (mask // chips))
            packed[pl.ds(pl.multiple_of(at * depth, depth), depth), :] = sources[s][
                mask
            ].astype(jnp.float32)
    for a in range(3):
        conv1[a] = packed[192 * a : 192 * a + 192, :]
        for n in range(2):
            at = 576 + 384 * (2 * a + n)
            conv2[a, :, n * 128 : (n + 1) * 128] = packed[at : at + 384, :]
    up[...] = packed[2880:3136, :]
    skip[...] = packed[3136:3264, :]
    out[...] = packed[3264:3272, :]


def unpack_kernel(orders, bounds, chips, block, place, *refs):
    parts = len(orders)
    sources = [refs[4 * p : 4 * p + 4] for p in range(parts)]
    little = refs[4 * parts : 4 * parts + 2]
    out, *small = refs[4 * parts + 2 : 4 * parts + 8]
    gathered, ready, packed, sems = refs[4 * parts + 8 :]
    tile, half = place[0], place[1]
    chip, core = tile >> 1, tile & 1
    ones = [lax.broadcasted_iota(jnp.int32, (128, 128), n) for n in range(2)]
    identity = (ones[0] == ones[1]).astype(jnp.bfloat16)
    batches = [
        (p, n, min(2, bounds[p + 1] - n))
        for p in range(parts)
        for n in range(bounds[p], bounds[p + 1], 2)
    ]

    def copy(n):
        _, start, count = batches[n]
        return pltpu.make_async_copy(
            ready.at[n % 4, 0:count], out.at[start : start + count], sems.at[n % 4]
        )

    for n, (p, start, count) in enumerate(batches):
        entries = sources[p][0].shape[0]
        for s in range(4):
            for i in range(entries):
                index = i + entries * (s % 2)
                mask = sum(1 << d for q, d in enumerate(orders[p]) if (index >> q) & 1)
                whose = 2 * (chip ^ (mask % chips)) + (core ^ (s // 2))
                for g in range(count):
                    at = (start - bounds[p] + g) * block
                    gathered[
                        n % 4,
                        g,
                        half ^ (mask // chips),
                        pl.ds(pl.multiple_of(whose * block, block), block),
                        :,
                    ] = sources[p][s][i, at : at + block, :]
        if n >= 4:
            copy(n - 4).wait()
        for g in range(count):
            for u in range(2):
                ready[n % 4, g, u * 128 : (u + 1) * 128, :] = dot(
                    identity, gathered[n % 4, g, u], NT
                )
        copy(n).start()
    write_small(chips, little, packed, small, chip, core, half)
    for n in range(max(0, len(batches) - 4), len(batches)):
        copy(n).wait()


def unpack(place, sources, small, orders, bounds, chips, block, packed_rows):
    wide = 2 * chips * block
    operands = [array for group in sources for array in group] + small
    shapes = [(TAPS * TAPS, 256, wide), (3, 192, 128), (3, 384, 256), (256, 128), (128, 128)]
    shapes.append((K, 128))
    return pl.pallas_call(
        functools.partial(unpack_kernel, orders, bounds, chips, block),
        out_shape=[jax.ShapeDtypeStruct(shape, jnp.float32) for shape in shapes],
        in_specs=[SMEM] + [VMEM] * len(operands),
        out_specs=[ANY] + [VMEM] * 5,
        scratch_shapes=[
            pltpu.VMEM((4, 2, 2, wide, 128), jnp.bfloat16),
            pltpu.VMEM((4, 2, 256, wide), jnp.float32),
            pltpu.VMEM((packed_rows, 128), jnp.float32),
            pltpu.SemaphoreType.DMA((4,)),
        ],
        compiler_params=params(56),
        cost_estimate=LIGHT,
        name="context_out",
    )(place, *operands)


def fold_small(packed, chips, first):
    t, _, half = position()
    steps = [(1, 0, t & 1)]
    for d in range(bits(chips)):
        steps.append((2 << d, 0, (t >> (d + 1)) & 1))
    steps.append((0, 1, half))
    for tile_mask, dp_mask, bit in steps:
        pairs = packed.reshape(2, packed.shape[0] // 2, 128)
        mine = lax.dynamic_index_in_dim(pairs, bit, 0, False)
        theirs = lax.dynamic_index_in_dim(pairs, 1 - bit, 0, False).astype(jnp.bfloat16)
        packed = mine + flip(theirs, tile_mask, dp_mask).astype(jnp.float32)
        if tile_mask == 1:
            packed, first = lax.optimization_barrier((packed, first))
    return packed.astype(jnp.bfloat16), first


def sum_and_share(term, small, place, chips, block, scale, results, packed_rows):
    dims = bits(chips) + 1
    groups = TAPS * TAPS
    bounds = [groups * p // dims for p in range(dims + 1)]
    parts = [term[bounds[p] * block : bounds[p + 1] * block] for p in range(dims)]
    totals, mask = [part.astype(jnp.float32) for part in parts], 3
    little = small.astype(jnp.float32)
    while mask < lax.axis_size("dp"):
        parts = [total.astype(jnp.bfloat16) for total in totals]
        others = [flip(part, 0, mask) for part in parts]
        others[0], results = lax.optimization_barrier((others[0], results))
        totals = [
            part.astype(jnp.float32) + other.astype(jnp.float32)
            for part, other in zip(parts, others)
        ]
        small = little.astype(jnp.bfloat16)
        little = small.astype(jnp.float32) + flip(small, 0, mask).astype(jnp.float32)
        mask = 4 if mask == 3 else 2 * mask
    parts = [(total * scale).astype(jnp.bfloat16)[None] for total in totals]
    small = (little * scale).astype(jnp.bfloat16)[None]
    orders = [[(p + q) % dims for q in range(dims)] for p in range(dims)]

    def across(value, dim):
        return flip(value, 2 << dim, 0) if dim < dims - 1 else flip(value, 0, 1)

    for q in range(dims):
        small = jnp.concatenate([small, across(small, q)])
    small = [small, flip(small, 1, 0)]
    for q in range(dims - 1):
        others = [across(part, orders[p][q]) for p, part in enumerate(parts)]
        parts = [jnp.concatenate(pair) for pair in zip(parts, others)]
    last = [across(part, orders[p][-1]) for p, part in enumerate(parts)]
    near = [flip(part, 1, 0) for part in parts]
    far = [flip(part, 1, 0) for part in last]
    sources = list(zip(parts, last, near, far))
    target, *small = unpack(place, sources, small, orders, bounds, chips, block, packed_rows)
    return target, small, results


def dot(lhs, rhs, dims=((1,), (0,))):
    return lax.dot_general(lhs, rhs, (dims, ((), ())), preferred_element_type=jnp.float32)


NT = ((1,), (1,))
TN = ((0,), (0,))


def encode_kernel(image, halo, weight1, weight2, taps, slope1, features, slope2, odd):
    rows, pairs = image.shape[0] // 2, image.shape[1]
    empty = jnp.zeros((pairs + 16, 256), jnp.bfloat16)

    def line(n):
        if n < 0:
            return empty
        return jnp.concatenate([halo[n], image[n]], axis=0)

    lhs = jnp.concatenate(
        [
            jnp.concatenate([line(2 * i + a - 1) for i in range(rows)], axis=0)
            for a in range(3)
        ],
        axis=1,
    )
    none = jnp.zeros((64, 128), jnp.bfloat16)
    rhs = []
    for a in range(3):
        for_odd = jnp.concatenate([none, weight1[a]], axis=0)
        for_even = jnp.concatenate([weight1[a, 64:], none, none], axis=0)
        for_next = jnp.concatenate([none, none, none, weight1[a, :64]], axis=0)
        rhs.append(jnp.concatenate([for_odd, for_even, for_next], axis=1))
    result = dot(lhs, jnp.concatenate(rhs, axis=0)).reshape(rows, pairs + 16, 384)
    odd[...] = result[:, :, 256:384]
    even_pre = result[:, 16:, 128:256] + odd[:, 15 : 15 + pairs, :]
    gate = jax.nn.sigmoid(even_pre)
    value = even_pre * gate
    taps[:, :, 128:256] = value.astype(jnp.bfloat16)
    slope1[:, :, 0:128] = gate + value * (1.0 - gate)
    odd_pre = result[:, :, 0:128]
    gate = jax.nn.sigmoid(odd_pre)
    value = odd_pre * gate
    odd[...] = value
    taps[:, :, 256:384] = value[:, 16:].astype(jnp.bfloat16)
    slope1[:, :, 128:256] = (gate + value * (1.0 - gate))[:, 16:]
    taps[:, :, 0:128] = odd[:, 15 : 15 + pairs, :].astype(jnp.bfloat16)
    empty = jnp.zeros((pairs, 384), jnp.bfloat16)
    lhs = jnp.concatenate(
        [
            jnp.concatenate(
                [
                    empty if 2 * i + a < 1 else taps[2 * i + a - 1]
                    for i in range(rows // 2)
                ],
                axis=0,
            )
            for a in range(3)
        ],
        axis=1,
    )
    pre = dot(lhs, weight2[...].reshape(1152, 256))
    gate = jax.nn.sigmoid(pre)
    value = pre * gate
    features[...] = value.astype(jnp.bfloat16).reshape(features.shape)
    slope2[...] = (gate + value * (1.0 - gate)).reshape(slope2.shape)


def encode(image, halo, weight1, weight2):
    rows, pairs = image.shape[0] // 2, image.shape[1]
    bf16, f32 = jnp.bfloat16, jnp.float32
    return pl.pallas_call(
        encode_kernel,
        out_shape=[
            jax.ShapeDtypeStruct((rows, pairs, 384), bf16),
            jax.ShapeDtypeStruct((rows, pairs, 256), f32),
            jax.ShapeDtypeStruct((rows // 2, pairs, 256), bf16),
            jax.ShapeDtypeStruct((rows // 2, pairs, 256), f32),
        ],
        in_specs=[VMEM] * 4,
        out_specs=[VMEM] * 4,
        scratch_shapes=[pltpu.VMEM((rows, pairs + 16, 128), f32)],
        compiler_params=params(56),
        cost_estimate=LIGHT,
        name="encode",
    )(image, halo, weight1, weight2)


def widen(wide, left, middle, right):
    width = middle.shape[1]
    wide[:, 0:48, :] = left[...]
    wide[:, 48 : 48 + width, :] = middle[...]
    wide[:, 48 + width : 96 + width, :] = right[...]


def decode_kernel(
    chips,
    block,
    place,
    left,
    features,
    right,
    weight,
    taps,
    labels,
    up,
    skip,
    classes,
    logits,
    gradient,
    mine,
    theirs,
    context,
    pooled,
    grad_decoder,
    out_term,
    wide,
    total,
    turned,
):
    rows, width = features.shape[0], features.shape[1]
    step = pl.program_id(0)

    @pl.when(step == 0)
    def _():
        widen(wide, left, features, right)
        total[...] = jnp.zeros_like(total)

    for a in range(TAPS):

        @pl.when(step == a)
        def _(a=a):
            low, high = max(0, 3 - a), min(rows, rows + 3 - a)
            lhs = jnp.concatenate(
                [
                    wide[
                        low + a - 3 : high + a - 3,
                        b * COLUMN_SPREAD : b * COLUMN_SPREAD + width,
                        :,
                    ].reshape((high - low) * width, 256)
                    for b in range(TAPS)
                ],
                axis=1,
            )
            total[low * width : high * width, :] += dot(lhs, weight[0])

    @pl.when(step == TAPS - 1)
    def _():
        pixels = rows * width
        pre = total[...]
        gate = jax.nn.sigmoid(pre)
        value = pre * gate
        total[...] = gate + value * (1.0 - gate)
        mixed = features[...].reshape(pixels, 256).astype(jnp.float32) + value
        mixed = mixed.astype(jnp.bfloat16)
        context[...] = mixed
        coarse = dot(mixed, up[...])
        pool = jnp.zeros((pixels, 128), jnp.float32)
        outer = jnp.zeros((K, 128), jnp.float32)
        kinds = lax.broadcasted_iota(jnp.int32, (K, pixels), 0).astype(jnp.float32)
        source, place_at = [lax.broadcasted_iota(jnp.int32, (256, 256), n) for n in range(2)]
        split = (source == 2 * (place_at & 127) + (place_at >> 7)).astype(jnp.bfloat16)
        parted = dot(labels[...].astype(jnp.float32).astype(jnp.bfloat16), split)
        for p in range(2):
            for q in range(2):
                fine = jnp.concatenate(
                    [taps[2 * i + q, :, 128 + 128 * p : 256 + 128 * p] for i in range(rows)],
                    axis=0,
                )
                pre = dot(fine, skip[...]) + coarse
                gate = jax.nn.sigmoid(pre)
                value = pre * gate
                decoded = value.astype(jnp.bfloat16)
                scores = dot(classes[...], decoded, NT)
                logits[p, q] = scores
                wanted = jnp.concatenate(
                    [
                        parted[2 * i + q : 2 * i + q + 1, p * 128 : (p + 1) * 128]
                        for i in range(rows)
                    ],
                    axis=1,
                )
                target = (kinds == wanted).astype(jnp.float32)
                grad = (jax.nn.sigmoid(scores) - target).astype(jnp.bfloat16)
                outer += dot(grad, decoded)
                back = dot(grad, classes[...], TN) * (gate + value * (1.0 - gate))
                back = back.astype(jnp.bfloat16)
                grad_decoder[p, q] = back
                pool += back.astype(jnp.float32)
        out_term[...] = outer
        small = pool.astype(jnp.bfloat16)
        pooled[...] = small
        result = dot(small, up[...], NT) * total[...]
        gradient[...] = result.astype(jnp.bfloat16).reshape(gradient.shape)
        for i in range(rows):
            line = result[i * width : (i + 1) * width].T.astype(jnp.bfloat16)
            turned[:, i] = line.reshape(2 * chips, block, width)
        chip, core = place[0] >> 1, place[0] & 1
        for mask in range(chips):
            mine[mask] = turned[2 * (chip ^ mask) + core]
            theirs[mask] = turned[2 * (chip ^ mask) + 1 - core]


def whole(shape):
    return pl.BlockSpec(shape, lambda n: (0,) * len(shape))


def decode(place, left, features, right, weight, taps, labels, up, skip, classes, chips):
    rows, width = features.shape[0], features.shape[1]
    pixels = rows * width
    block = 128 // chips
    bf16, f32 = jnp.bfloat16, jnp.float32
    operands = (left, features, right, weight, taps, labels, up, skip, classes)
    specs = [whole(x.shape) for x in operands]
    specs[3] = pl.BlockSpec((1, *weight.shape[1:]), lambda n: (n, 0, 0))
    outs = [
        jax.ShapeDtypeStruct((2, 2, K, pixels), f32),
        jax.ShapeDtypeStruct((rows, width, 256), bf16),
        jax.ShapeDtypeStruct((chips, rows, block, width), bf16),
        jax.ShapeDtypeStruct((chips, rows, block, width), bf16),
        jax.ShapeDtypeStruct((pixels, 256), bf16),
        jax.ShapeDtypeStruct((pixels, 128), bf16),
        jax.ShapeDtypeStruct((2, 2, pixels, 128), bf16),
        jax.ShapeDtypeStruct((K, 128), f32),
    ]
    return pl.pallas_call(
        functools.partial(decode_kernel, chips, block),
        out_shape=outs,
        grid=(TAPS,),
        in_specs=[SMEM, *specs],
        out_specs=[whole(x.shape) for x in outs],
        scratch_shapes=[
            pltpu.VMEM((rows, width + 96, 256), bf16),
            pltpu.VMEM((pixels, 256), f32),
            pltpu.VMEM((2 * chips, rows, block, width), bf16),
        ],
        compiler_params=params(56),
        cost_estimate=LIGHT,
        name="decode",
    )(place, *operands)


def back_kernel(
    left,
    gradient,
    right,
    weight,
    pooled,
    up,
    slope2,
    taps,
    grad_decoder,
    skip,
    weight2,
    context,
    partial,
    edge,
    term2,
    up_term,
    skip_term,
    wide,
    total,
    before,
):
    rows, width = gradient.shape[0], gradient.shape[1]
    pixels = rows * width
    step = pl.program_id(0)

    @pl.when(step == 0)
    def _():
        widen(wide, left, gradient, right)
        total[...] = dot(pooled[...], up[...], NT)

    for a in range(TAPS):

        @pl.when(step == a)
        def _(a=a):
            low, high = max(0, a - 3), min(rows, rows + a - 3)
            result = None
            for b in range(TAPS):
                at = (6 - b) * COLUMN_SPREAD
                lhs = wide[low - a + 3 : high - a + 3, at : at + width, :]
                lhs = lhs.reshape((high - low) * width, 256)
                one = dot(lhs, weight[0, b * 256 : (b + 1) * 256, :], NT)
                result = one if result is None else result + one
            total[low * width : high * width, :] += result

    @pl.when(step == TAPS - 1)
    def _():
        grad = (total[...] * slope2[...].reshape(pixels, 256)).astype(jnp.bfloat16)
        up_term[...] = dot(context[...], pooled[...], TN)
        backs = []
        for a in range(3):
            first = 1 if a == 0 else 0
            lhs = jnp.concatenate(
                [taps[2 * i + a - 1] for i in range(first, rows)], axis=0
            )
            term2[a] = dot(lhs, grad[first * width :], TN)
            backs.append(dot(grad, weight2[a], NT))
        skips = jnp.zeros((128, 128), jnp.float32)
        for p in range(2):
            for q in range(2):
                fine = jnp.concatenate(
                    [taps[2 * i + q, :, 128 + 128 * p : 256 + 128 * p] for i in range(rows)],
                    axis=0,
                )
                skips += dot(fine, grad_decoder[p, q], TN)
                through = dot(grad_decoder[p, q], skip[...], NT)
                for i in range(rows):
                    partial[2 * i + q, :, p * 128 : (p + 1) * 128] = through[
                        i * width : (i + 1) * width
                    ]
        skip_term[...] = skips
        before[:, width : width + 8, :] = jnp.zeros((2 * rows, 8, 128), jnp.float32)
        for i in range(rows):
            here = slice(i * width, (i + 1) * width)
            even = backs[1][here]
            odd = backs[2][here]
            if i + 1 < rows:
                odd = odd + backs[0][(i + 1) * width : (i + 2) * width]
            for q, line in enumerate((even, odd)):
                before[2 * i + q, 0:width, :] = line[:, 0:128]
                partial[2 * i + q, :, 0:128] += line[:, 128:256]
                partial[2 * i + q, :, 128:256] += (
                    line[:, 256:384] + before[2 * i + q, 1 : width + 1, :]
                )
        edge[...] = before[:, 0:1, :]


def back(left, gradient, right, weight, pooled, up, slope2, taps, grads, skip, weight2, context):
    rows, width = gradient.shape[0], gradient.shape[1]
    pixels = rows * width
    bf16, f32 = jnp.bfloat16, jnp.float32
    operands = (
        left, gradient, right, weight, pooled, up, slope2, taps, grads, skip, weight2, context,
    )
    specs = [whole(x.shape) for x in operands]
    specs[3] = pl.BlockSpec((1, *weight.shape[1:]), lambda n: (n, 0, 0))
    outs = [
        jax.ShapeDtypeStruct((2 * rows, width, 256), f32),
        jax.ShapeDtypeStruct((2 * rows, 1, 128), f32),
        jax.ShapeDtypeStruct((3, 384, 256), f32),
        jax.ShapeDtypeStruct((256, 128), f32),
        jax.ShapeDtypeStruct((128, 128), f32),
    ]
    return pl.pallas_call(
        back_kernel,
        out_shape=outs,
        grid=(TAPS,),
        in_specs=specs,
        out_specs=[whole(x.shape) for x in outs],
        scratch_shapes=[
            pltpu.VMEM((rows, width + 96, 256), bf16),
            pltpu.VMEM((pixels, 256), f32),
            pltpu.VMEM((2 * rows, width + 8, 128), f32),
        ],
        compiler_params=params(56),
        cost_estimate=LIGHT,
        name="back",
    )(*operands)


def finish_kernel(
    partial, returned, slope1, image, halo, term2, up_term, skip_term, out_term, out, packed, shifted_up
):
    rows, width = partial.shape[0], partial.shape[1]
    last = lax.broadcasted_iota(jnp.int32, (rows, width, 128), 1) == width - 1
    even = partial[:, :, 0:128]
    odd = partial[:, :, 128:256] + jnp.where(last, returned[...], 0.0)
    for i in range(rows):
        out[i, pl.ds(0, width, stride=2), :] = even[i]
        out[i, pl.ds(1, width, stride=2), :] = odd[i]
    even = even * slope1[:, :, 0:128]
    odd = (odd * slope1[:, :, 128:256]).astype(jnp.bfloat16)
    shifted_up[:, 0:16, :] = jnp.zeros((rows, 16, 128), jnp.float32)
    shifted_up[:, width + 8 : width + 16, :] = jnp.zeros((rows, 8, 128), jnp.float32)
    shifted_up[:, 15 : 15 + width, :] = even
    even = even.astype(jnp.bfloat16)
    moved = shifted_up[...].astype(jnp.bfloat16)
    rhs = jnp.concatenate([odd, even, moved[:, 16:]], axis=2)
    for a in range(3):
        first = 1 if a == 0 else 0
        lines = [2 * i + a - 1 for i in range(first, rows)]
        lhs = jnp.concatenate([image[n] for n in lines], axis=0)
        result = dot(lhs, rhs[first:].reshape((rows - first) * width, 384), TN)
        side = jnp.concatenate([halo[n] for n in lines], axis=0)
        outer = dot(side, moved[first:, 0:16].reshape((rows - first) * 16, 128), TN)
        at = 192 * a
        packed[at : at + 64, :] = (
            result[192:256, 256:384] + outer[192:256] + result[64:128, 0:128]
        )
        packed[at + 64 : at + 128, :] = result[0:64, 128:256] + result[128:192, 0:128]
        packed[at + 128 : at + 192, :] = result[64:128, 128:256] + result[192:256, 0:128]
        for n in range(2):
            at = 576 + 384 * (2 * a + n)
            packed[at : at + 384, :] = term2[a, :, n * 128 : (n + 1) * 128]
    packed[2880:3136, :] = up_term[...]
    packed[3136:3264, :] = skip_term[...]
    packed[3264:3272, :] = out_term[...]
    packed[3272:, :] = jnp.zeros((packed.shape[0] - 3272, 128), jnp.float32)


def finish(partial, returned, slope1, image, halo, terms, packed_rows):
    rows, width = partial.shape[0], partial.shape[1]
    f32 = jnp.float32
    return pl.pallas_call(
        finish_kernel,
        out_shape=[
            jax.ShapeDtypeStruct((rows, 2 * width, 128), f32),
            jax.ShapeDtypeStruct((packed_rows, 128), f32),
        ],
        in_specs=[VMEM] * 9,
        out_specs=[VMEM] * 2,
        scratch_shapes=[pltpu.VMEM((rows, width + 16, 128), f32)],
        compiler_params=params(56),
        cost_estimate=LIGHT,
        name="finish",
    )(partial, returned, slope1, image, halo, *terms)


def moved(block, distance):
    tiles = lax.axis_size("tile")
    route = [(i, i + distance) for i in range(tiles) if 0 <= i + distance < tiles]
    return lax.ppermute(block, "tile", route)


def edges(value):
    return moved(value[:, -48:], 1), moved(value[:, :48], -1)


def body(
    scan_pixels,
    labels,
    conv1_weight,
    conv2_weight,
    context_weight,
    up_weight,
    skip_weight,
    class_weight,
):
    bf16 = jnp.bfloat16
    tiles = lax.axis_size("tile")
    chips = tiles // 2
    t, _, half = position()
    place = jnp.stack([t, half]).astype(jnp.int32)
    lines, line_pairs, _ = scan_pixels[0].shape
    rows, width = lines // 4, line_pairs // 2
    corner = moved(scan_pixels[0, :, -2:, :].reshape(lines, 1, 256), 1)
    halo = jnp.concatenate([jnp.zeros((lines, 15, 256), bf16), corner], axis=1)
    image = scan_pixels[0].reshape(lines, width, 256)
    taps, slope1, features, slope2 = encode(image, halo, conv1_weight, conv2_weight)
    left, right = edges(features)
    logits, gradient, mine, theirs, context, pooled, grads, out_term = decode(
        place, left, features, right, context_weight, taps, labels[0],
        up_weight, skip_weight, class_weight, chips,
    )
    messages = pack(place, features, mine, flip(theirs, 1, 0))
    gradient, messages = lax.optimization_barrier((gradient, messages))

    def send(m, message):
        return flip(message, 2 * (m % chips), m // chips)

    own = [messages[0]] + [send(m, messages[m]) for m in range(1, 2 * chips)]
    left, right = edges(gradient)
    partial, edge, conv2_term, up_term, skip_term = back(
        left, gradient, right, context_weight, pooled, up_weight, slope2, taps, grads,
        skip_weight, conv2_weight, context,
    )
    returned = moved(edge, -1)
    partial, own = lax.optimization_barrier((partial, own))
    other = [flip(part, 1, 0) for part in own]
    packed_rows = -(-3272 // (64 * chips)) * 64 * chips
    grad_features, packed = finish(
        partial, returned, slope1, image, halo,
        (conv2_term, up_term, skip_term, out_term), packed_rows,
    )
    other, packed = lax.optimization_barrier((other, packed))
    block = mine.shape[2]
    context_term = wgrad(place, own, other, chips, rows, width, block)
    logits = logits.reshape(2, 2, K, rows, width).transpose(2, 3, 1, 4, 0)
    logits = logits.reshape(1, K, 2 * rows, 2 * width)
    grad_features = grad_features[None]
    scale = 1.0 / (lax.axis_size("dp") * tiles * 4 * rows * width)
    folded, context_term = fold_small(packed, chips, context_term)
    grad_context, small, logits = sum_and_share(
        context_term, folded, place, chips, block, scale, logits, packed_rows
    )
    return (
        logits,
        grad_features,
        small[0],
        small[1],
        grad_context.reshape(context_weight.shape),
        small[2],
        small[3],
        small[4],
    )


def solution(mesh):
    in_specs = (P("dp", None, "tile", None), P("dp", None, "tile"), P(), P(), P(), P(), P(), P())
    out_specs = (
        P("dp", None, None, "tile"),
        P("dp", None, "tile", None),
        P(),
        P(),
        P(),
        P(),
        P(),
        P(),
    )
    return jax.shard_map(body, mesh=mesh, in_specs=in_specs, out_specs=out_specs, check_vma=False)
```

```python
import functools

import jax
import jax.numpy as jnp
from jax import lax
from jax.experimental import pallas as pl
from jax.experimental.pallas import tpu as pltpu
from jax.sharding import PartitionSpec as P

K = 8
COLUMN_SPREAD = 16
TAPS = 7
BOTH = ("tile", "dp")
VMEM = pl.BlockSpec(memory_space=pltpu.VMEM)
SMEM = pl.BlockSpec(memory_space=pltpu.SMEM)
ANY = pl.BlockSpec(memory_space=pl.ANY)

LIGHT = pl.CostEstimate(flops=1000, bytes_accessed=1000, transcendentals=0)


def params(mebibytes):
    return pltpu.CompilerParams(vmem_limit_bytes=mebibytes * 1024 * 1024)


def flip(value, tile_mask, dp_mask):
    tiles, slabs = lax.axis_size("tile"), lax.axis_size("dp")
    route = [
        (t * slabs + z, (t ^ tile_mask) * slabs + (z ^ dp_mask))
        for t in range(tiles)
        for z in range(slabs)
    ]
    return lax.ppermute(value, BOTH, route)


def bits(count):
    return count.bit_length() - 1


def position():
    t, z = lax.axis_index("tile"), lax.axis_index("dp")
    return t, z, (z & 1) ^ ((z >> 1) & 1)


def row_pairs(rows):
    out = []
    for first in range(0, rows, 2):
        pair = [i for i in (first, first + 1) if i < rows]
        low = max(0, pair[0] - 3)
        high = min(rows, pair[-1] + 4)
        out.append((pair, low, high))
    return out


def wgrad_kernel(chips, rows, width, block, place, *refs):
    masks = 2 * chips
    own, other = refs[:masks], refs[masks : 2 * masks]
    out, features, wide, stacked, total = refs[2 * masks :]
    chip, core = place[0] >> 1, place[0] & 1
    columns = 2 * chips * width
    for m in range(masks):
        slab, mask = m // chips, m % chips
        for k in range(2):
            tile = 2 * (chip ^ mask) + (core ^ k)
            at = pl.multiple_of(tile * width, width)
            for i in range(rows):
                start = (rows * (width + k * block)) + i * block
                features[slab, i, pl.ds(at, width), :] = (own, other)[k][m][
                    i * width : (i + 1) * width, :
                ]
                wide[slab, i, :, pl.ds(pl.multiple_of(at + 128, 128), width)] = own[m][
                    start : start + block, :
                ].astype(jnp.float32)
    for slab in range(2):
        for i in range(rows):
            edge = jnp.zeros((block, 128), jnp.float32)
            wide[slab, i, :, 0:128] = edge
            wide[slab, i, :, 128 + columns : 256 + columns] = edge
            for b in range(TAPS):
                start = 128 - (b - 3) * COLUMN_SPREAD
                stacked[slab, i, b * block : (b + 1) * block, :] = wide[
                    slab, i, :, start : start + columns
                ].astype(jnp.bfloat16)
    total[...] = jnp.zeros_like(total)
    for slab in range(2):
        for pair, low, high in row_pairs(rows):
            lhs = stacked[slab, low:high].reshape((high - low) * TAPS * block, columns)
            rhs = jnp.concatenate([features[slab, i] for i in pair], axis=-1)
            result = jnp.dot(lhs, rhs, preferred_element_type=jnp.float32)
            for n, i in enumerate(pair):
                for j in range(low, high):
                    a = i - j + 3
                    if 0 <= a < TAPS:
                        total[a] += result[
                            (j - low) * TAPS * block : (j - low + 1) * TAPS * block,
                            n * 128 : (n + 1) * 128,
                        ]
    out[...] = total[...].reshape(out.shape).astype(jnp.bfloat16)


def wgrad(place, own, other, chips, rows, width, block):
    columns = 2 * chips * width
    return pl.pallas_call(
        functools.partial(wgrad_kernel, chips, rows, width, block),
        out_shape=jax.ShapeDtypeStruct((TAPS * TAPS * block, 128), jnp.bfloat16),
        in_specs=[SMEM] + [VMEM] * (2 * len(own)),
        out_specs=VMEM,
        scratch_shapes=[
            pltpu.VMEM((2, rows, columns, 128), jnp.bfloat16),
            pltpu.VMEM((2, rows, block, columns + 256), jnp.float32),
            pltpu.VMEM((2, rows, TAPS * block, columns), jnp.bfloat16),
            pltpu.VMEM((TAPS, TAPS * block, 128), jnp.float32),
        ],
        compiler_params=params(56),
        cost_estimate=LIGHT,
        name="context_term",
    )(place, *own, *other)


def pack_kernel(chips, rows, width, block, place, features, mine, theirs, *messages):
    half = place[1]
    for m, message in enumerate(messages):
        mask = m % chips
        at = pl.multiple_of((half ^ (m // chips)) * 128, 128)
        for i in range(rows):
            message[i * width : (i + 1) * width, :] = features[i, :, pl.ds(at, 128)]
            for k, part in enumerate((mine, theirs)):
                start = rows * (width + k * block) + i * block
                message[start : start + block, :] = part[mask, i]


def pack(place, features, mine, theirs):
    rows, width = features.shape[0], features.shape[1]
    chips, block = mine.shape[0], mine.shape[2]
    shape = jax.ShapeDtypeStruct((rows * (width + 2 * block), 128), jnp.bfloat16)
    return pl.pallas_call(
        functools.partial(pack_kernel, chips, rows, width, block),
        out_shape=[shape] * (2 * chips),
        in_specs=[SMEM] + [VMEM] * 3,
        out_specs=[VMEM] * (2 * chips),
        compiler_params=params(56),
        cost_estimate=LIGHT,
        name="pack",
    )(place, features, mine, theirs)


def write_small(chips, sources, packed, outs, chip, core, half):
    conv1, conv2, up, skip, out = outs
    depth = packed.shape[0] // (4 * chips)
    for s in range(2):
        for mask in range(2 * chips):
            whose = chip ^ (mask % chips)
            at = core ^ s
            for d in range(bits(chips)):
                at = 2 * at + ((whose >> d) & 1)
            at = 2 * at + (half ^ (mask // chips))
            packed[pl.ds(pl.multiple_of(at * depth, depth), depth), :] = sources[s][
                mask
            ].astype(jnp.float32)
    for a in range(3):
        conv1[a] = packed[192 * a : 192 * a + 192, :]
        for n in range(2):
            at = 576 + 384 * (2 * a + n)
            conv2[a, :, n * 128 : (n + 1) * 128] = packed[at : at + 384, :]
    up[...] = packed[2880:3136, :]
    skip[...] = packed[3136:3264, :]
    out[...] = packed[3264:3272, :]


def unpack_kernel(orders, bounds, chips, block, place, *refs):
    parts = len(orders)
    sources = [refs[4 * p : 4 * p + 4] for p in range(parts)]
    little = refs[4 * parts : 4 * parts + 2]
    out, *small = refs[4 * parts + 2 : 4 * parts + 8]
    gathered, ready, packed, sems, loaded, *held = refs[4 * parts + 8 :]
    loads = [
        pltpu.make_async_copy(refs[n], held[n], loaded.at[n]) for n in range(4 * parts)
    ]
    for load in loads:
        load.start()
    sources = [held[4 * p : 4 * p + 4] for p in range(parts)]
    tile, half = place[0], place[1]
    chip, core = tile >> 1, tile & 1
    ones = [lax.broadcasted_iota(jnp.int32, (256, 256), n) for n in range(2)]
    identity = (ones[0] == ones[1]).astype(jnp.bfloat16)
    batches = [
        (p, n, min(2, bounds[p + 1] - n))
        for p in range(parts)
        for n in range(bounds[p], bounds[p + 1], 2)
    ]

    def copy(n):
        _, start, count = batches[n]
        return pltpu.make_async_copy(
            ready.at[n % 4, 0:count], out.at[start : start + count], sems.at[n % 4]
        )

    for n, (p, start, count) in enumerate(batches):
        if start == bounds[p]:
            for load in loads[4 * p : 4 * p + 4]:
                load.wait()
        entries = sources[p][0].shape[0]
        for s in range(4):
            for i in range(entries):
                index = i + entries * (s % 2)
                mask = sum(1 << d for q, d in enumerate(orders[p]) if (index >> q) & 1)
                whose = 2 * (chip ^ (mask % chips)) + (core ^ (s // 2))
                for g in range(count):
                    at = (start - bounds[p] + g) * block
                    gathered[
                        n % 4,
                        g,
                        pl.ds(pl.multiple_of(whose * block, block), block),
                        pl.ds(pl.multiple_of((half ^ (mask // chips)) * 128, 128), 128),
                    ] = sources[p][s][i, at : at + block, :]
        if n >= 4:
            copy(n - 4).wait()
        for g in range(count):
            ready[n % 4, g] = dot(identity, gathered[n % 4, g], NT)
        copy(n).start()
    write_small(chips, little, packed, small, chip, core, half)
    for n in range(max(0, len(batches) - 4), len(batches)):
        copy(n).wait()


def unpack(place, sources, small, orders, bounds, chips, block, packed_rows):
    wide = 2 * chips * block
    operands = [array for group in sources for array in group] + small
    shapes = [(TAPS * TAPS, 256, wide), (3, 192, 128), (3, 384, 256), (256, 128), (128, 128)]
    shapes.append((K, 128))
    return pl.pallas_call(
        functools.partial(unpack_kernel, orders, bounds, chips, block),
        out_shape=[jax.ShapeDtypeStruct(shape, jnp.float32) for shape in shapes],
        in_specs=[SMEM] + [ANY] * (len(operands) - 2) + [VMEM] * 2,
        out_specs=[ANY] + [VMEM] * 5,
        scratch_shapes=[
            pltpu.VMEM((4, 2, wide, 256), jnp.bfloat16),
            pltpu.VMEM((4, 2, 256, wide), jnp.float32),
            pltpu.VMEM((packed_rows, 128), jnp.float32),
            pltpu.SemaphoreType.DMA((4,)),
            pltpu.SemaphoreType.DMA((len(operands) - 2,)),
            *[pltpu.VMEM(x.shape, x.dtype) for x in operands[:-2]],
        ],
        compiler_params=params(56),
        cost_estimate=LIGHT,
        name="context_out",
    )(place, *operands)


def fold_small(packed, chips, first):
    t, _, half = position()
    steps = [(1, 0, t & 1)]
    for d in range(bits(chips)):
        steps.append((2 << d, 0, (t >> (d + 1)) & 1))
    steps.append((0, 1, half))
    for tile_mask, dp_mask, bit in steps:
        pairs = packed.reshape(2, packed.shape[0] // 2, 128)
        mine = lax.dynamic_index_in_dim(pairs, bit, 0, False)
        theirs = lax.dynamic_index_in_dim(pairs, 1 - bit, 0, False).astype(jnp.bfloat16)
        packed = mine + flip(theirs, tile_mask, dp_mask).astype(jnp.float32)
        if tile_mask == 1:
            packed, first = lax.optimization_barrier((packed, first))
    return packed.astype(jnp.bfloat16), first


def sum_and_share(term, small, place, chips, block, scale, results, packed_rows):
    dims = bits(chips) + 1
    groups = TAPS * TAPS
    bounds = [groups * p // dims for p in range(dims + 1)]
    parts = [term[bounds[p] * block : bounds[p + 1] * block] for p in range(dims)]
    totals, mask = [part.astype(jnp.float32) for part in parts], 3
    little = small.astype(jnp.float32)
    while mask < lax.axis_size("dp"):
        parts = [total.astype(jnp.bfloat16) for total in totals]
        others = [flip(part, 0, mask) for part in parts]
        others[0], results = lax.optimization_barrier((others[0], results))
        totals = [
            part.astype(jnp.float32) + other.astype(jnp.float32)
            for part, other in zip(parts, others)
        ]
        small = little.astype(jnp.bfloat16)
        little = small.astype(jnp.float32) + flip(small, 0, mask).astype(jnp.float32)
        mask = 4 if mask == 3 else 2 * mask
    parts = [(total * scale).astype(jnp.bfloat16)[None] for total in totals]
    small = (little * scale).astype(jnp.bfloat16)[None]
    orders = [[(p + q) % dims for q in range(dims)] for p in range(dims)]

    def across(value, dim):
        return flip(value, 2 << dim, 0) if dim < dims - 1 else flip(value, 0, 1)

    for q in range(dims):
        small = jnp.concatenate([small, across(small, q)])
    small = [small, flip(small, 1, 0)]
    for q in range(dims - 1):
        others = [across(part, orders[p][q]) for p, part in enumerate(parts)]
        parts = [jnp.concatenate(pair) for pair in zip(parts, others)]
    last = [across(part, orders[p][-1]) for p, part in enumerate(parts)]
    near = [flip(part, 1, 0) for part in parts]
    far = [flip(part, 1, 0) for part in last]
    sources = list(zip(parts, last, near, far))
    target, *small = unpack(place, sources, small, orders, bounds, chips, block, packed_rows)
    return target, small, results


def dot(lhs, rhs, dims=((1,), (0,))):
    return lax.dot_general(lhs, rhs, (dims, ((), ())), preferred_element_type=jnp.float32)


NT = ((1,), (1,))
TN = ((0,), (0,))


def encode_kernel(image, halo, weight1, weight2, taps, slope1, features, slope2, odd):
    rows, pairs = image.shape[0] // 2, image.shape[1]
    empty = jnp.zeros((pairs + 16, 256), jnp.bfloat16)

    def line(n):
        if n < 0:
            return empty
        return jnp.concatenate([halo[n], image[n]], axis=0)

    lhs = jnp.concatenate(
        [
            jnp.concatenate([line(2 * i + a - 1) for i in range(rows)], axis=0)
            for a in range(3)
        ],
        axis=1,
    )
    none = jnp.zeros((64, 128), jnp.bfloat16)
    rhs = []
    for a in range(3):
        for_odd = jnp.concatenate([none, weight1[a]], axis=0)
        for_even = jnp.concatenate([weight1[a, 64:], none, none], axis=0)
        for_next = jnp.concatenate([none, none, none, weight1[a, :64]], axis=0)
        rhs.append(jnp.concatenate([for_odd, for_even, for_next], axis=1))
    result = dot(lhs, jnp.concatenate(rhs, axis=0)).reshape(rows, pairs + 16, 384)
    odd[...] = result[:, :, 256:384]
    even_pre = result[:, 16:, 128:256] + odd[:, 15 : 15 + pairs, :]
    gate = jax.nn.sigmoid(even_pre)
    value = even_pre * gate
    taps[:, :, 128:256] = value.astype(jnp.bfloat16)
    slope1[:, :, 0:128] = gate + value * (1.0 - gate)
    odd_pre = result[:, :, 0:128]
    gate = jax.nn.sigmoid(odd_pre)
    value = odd_pre * gate
    odd[...] = value
    taps[:, :, 256:384] = value[:, 16:].astype(jnp.bfloat16)
    slope1[:, :, 128:256] = (gate + value * (1.0 - gate))[:, 16:]
    taps[:, :, 0:128] = odd[:, 15 : 15 + pairs, :].astype(jnp.bfloat16)
    empty = jnp.zeros((pairs, 384), jnp.bfloat16)
    lhs = jnp.concatenate(
        [
            jnp.concatenate(
                [
                    empty if 2 * i + a < 1 else taps[2 * i + a - 1]
                    for i in range(rows // 2)
                ],
                axis=0,
            )
            for a in range(3)
        ],
        axis=1,
    )
    pre = dot(lhs, weight2[...].reshape(1152, 256))
    gate = jax.nn.sigmoid(pre)
    value = pre * gate
    features[...] = value.astype(jnp.bfloat16).reshape(features.shape)
    slope2[...] = (gate + value * (1.0 - gate)).reshape(slope2.shape)


def encode(image, halo, weight1, weight2):
    rows, pairs = image.shape[0] // 2, image.shape[1]
    bf16, f32 = jnp.bfloat16, jnp.float32
    return pl.pallas_call(
        encode_kernel,
        out_shape=[
            jax.ShapeDtypeStruct((rows, pairs, 384), bf16),
            jax.ShapeDtypeStruct((rows, pairs, 256), f32),
            jax.ShapeDtypeStruct((rows // 2, pairs, 256), bf16),
            jax.ShapeDtypeStruct((rows // 2, pairs, 256), f32),
        ],
        in_specs=[VMEM] * 4,
        out_specs=[VMEM] * 4,
        scratch_shapes=[pltpu.VMEM((rows, pairs + 16, 128), f32)],
        compiler_params=params(56),
        cost_estimate=LIGHT,
        name="encode",
    )(image, halo, weight1, weight2)


def widen(wide, left, middle, right):
    width = middle.shape[1]
    wide[:, 0:48, :] = left[...]
    wide[:, 48 : 48 + width, :] = middle[...]
    wide[:, 48 + width : 96 + width, :] = right[...]


def decode_kernel(
    chips,
    block,
    place,
    left,
    features,
    right,
    weight,
    taps,
    labels,
    up,
    skip,
    classes,
    logits,
    gradient,
    mine,
    theirs,
    context,
    pooled,
    grad_decoder,
    out_term,
    wide,
    total,
    turned,
):
    rows, width = features.shape[0], features.shape[1]
    step = pl.program_id(0)

    @pl.when(step == 0)
    def _():
        widen(wide, left, features, right)
        total[...] = jnp.zeros_like(total)

    for a in range(TAPS):

        @pl.when(step == a)
        def _(a=a):
            low, high = max(0, 3 - a), min(rows, rows + 3 - a)
            lhs = jnp.concatenate(
                [
                    wide[
                        low + a - 3 : high + a - 3,
                        b * COLUMN_SPREAD : b * COLUMN_SPREAD + width,
                        :,
                    ].reshape((high - low) * width, 256)
                    for b in range(TAPS)
                ],
                axis=1,
            )
            total[low * width : high * width, :] += dot(lhs, weight[0])

    @pl.when(step == TAPS - 1)
    def _():
        pixels = rows * width
        pre = total[...]
        gate = jax.nn.sigmoid(pre)
        value = pre * gate
        total[...] = gate + value * (1.0 - gate)
        mixed = features[...].reshape(pixels, 256).astype(jnp.float32) + value
        mixed = mixed.astype(jnp.bfloat16)
        context[...] = mixed
        coarse = dot(mixed, up[...])
        pool = jnp.zeros((pixels, 128), jnp.float32)
        outer = jnp.zeros((K, 128), jnp.float32)
        kinds = lax.broadcasted_iota(jnp.int32, (K, pixels), 0).astype(jnp.float32)
        source, place_at = [lax.broadcasted_iota(jnp.int32, (256, 256), n) for n in range(2)]
        split = (source == 2 * (place_at & 127) + (place_at >> 7)).astype(jnp.bfloat16)
        parted = dot(labels[...].astype(jnp.float32).astype(jnp.bfloat16), split)
        for p in range(2):
            for q in range(2):
                fine = jnp.concatenate(
                    [taps[2 * i + q, :, 128 + 128 * p : 256 + 128 * p] for i in range(rows)],
                    axis=0,
                )
                pre = dot(fine, skip[...]) + coarse
                gate = jax.nn.sigmoid(pre)
                value = pre * gate
                decoded = value.astype(jnp.bfloat16)
                scores = dot(classes[...], decoded, NT)
                logits[p, q] = scores
                wanted = jnp.concatenate(
                    [
                        parted[2 * i + q : 2 * i + q + 1, p * 128 : (p + 1) * 128]
                        for i in range(rows)
                    ],
                    axis=1,
                )
                target = (kinds == wanted).astype(jnp.float32)
                grad = (jax.nn.sigmoid(scores) - target).astype(jnp.bfloat16)
                outer += dot(grad, decoded)
                back = dot(grad, classes[...], TN) * (gate + value * (1.0 - gate))
                back = back.astype(jnp.bfloat16)
                grad_decoder[p, q] = back
                pool += back.astype(jnp.float32)
        out_term[...] = outer
        small = pool.astype(jnp.bfloat16)
        pooled[...] = small
        result = dot(small, up[...], NT) * total[...]
        gradient[...] = result.astype(jnp.bfloat16).reshape(gradient.shape)
        for i in range(rows):
            line = result[i * width : (i + 1) * width].T.astype(jnp.bfloat16)
            turned[:, i] = line.reshape(2 * chips, block, width)
        chip, core = place[0] >> 1, place[0] & 1
        for mask in range(chips):
            mine[mask] = turned[2 * (chip ^ mask) + core]
            theirs[mask] = turned[2 * (chip ^ mask) + 1 - core]


def whole(shape):
    return pl.BlockSpec(shape, lambda n: (0,) * len(shape))


def decode(place, left, features, right, weight, taps, labels, up, skip, classes, chips):
    rows, width = features.shape[0], features.shape[1]
    pixels = rows * width
    block = 128 // chips
    bf16, f32 = jnp.bfloat16, jnp.float32
    operands = (left, features, right, weight, taps, labels, up, skip, classes)
    specs = [whole(x.shape) for x in operands]
    specs[3] = pl.BlockSpec((1, *weight.shape[1:]), lambda n: (n, 0, 0))
    outs = [
        jax.ShapeDtypeStruct((2, 2, K, pixels), f32),
        jax.ShapeDtypeStruct((rows, width, 256), bf16),
        jax.ShapeDtypeStruct((chips, rows, block, width), bf16),
        jax.ShapeDtypeStruct((chips, rows, block, width), bf16),
        jax.ShapeDtypeStruct((pixels, 256), bf16),
        jax.ShapeDtypeStruct((pixels, 128), bf16),
        jax.ShapeDtypeStruct((2, 2, pixels, 128), bf16),
        jax.ShapeDtypeStruct((K, 128), f32),
    ]
    return pl.pallas_call(
        functools.partial(decode_kernel, chips, block),
        out_shape=outs,
        grid=(TAPS,),
        in_specs=[SMEM, *specs],
        out_specs=[whole(x.shape) for x in outs],
        scratch_shapes=[
            pltpu.VMEM((rows, width + 96, 256), bf16),
            pltpu.VMEM((pixels, 256), f32),
            pltpu.VMEM((2 * chips, rows, block, width), bf16),
        ],
        compiler_params=params(56),
        cost_estimate=LIGHT,
        name="decode",
    )(place, *operands)


def back_kernel(
    left,
    gradient,
    right,
    weight,
    pooled,
    up,
    slope2,
    taps,
    grad_decoder,
    skip,
    weight2,
    context,
    partial,
    edge,
    term2,
    up_term,
    skip_term,
    wide,
    total,
    before,
):
    rows, width = gradient.shape[0], gradient.shape[1]
    pixels = rows * width
    step = pl.program_id(0)

    @pl.when(step == 0)
    def _():
        widen(wide, left, gradient, right)
        total[...] = dot(pooled[...], up[...], NT)

    for a in range(TAPS):

        @pl.when(step == a)
        def _(a=a):
            low, high = max(0, a - 3), min(rows, rows + a - 3)
            result = None
            for b in range(TAPS):
                at = (6 - b) * COLUMN_SPREAD
                lhs = wide[low - a + 3 : high - a + 3, at : at + width, :]
                lhs = lhs.reshape((high - low) * width, 256)
                one = dot(lhs, weight[0, b * 256 : (b + 1) * 256, :], NT)
                result = one if result is None else result + one
            total[low * width : high * width, :] += result

    @pl.when(step == TAPS - 1)
    def _():
        grad = (total[...] * slope2[...].reshape(pixels, 256)).astype(jnp.bfloat16)
        up_term[...] = dot(context[...], pooled[...], TN)
        backs = []
        for a in range(3):
            first = 1 if a == 0 else 0
            lhs = jnp.concatenate(
                [taps[2 * i + a - 1] for i in range(first, rows)], axis=0
            )
            term2[a] = dot(lhs, grad[first * width :], TN)
            backs.append(dot(grad, weight2[a], NT))
        skips = jnp.zeros((128, 128), jnp.float32)
        for p in range(2):
            for q in range(2):
                fine = jnp.concatenate(
                    [taps[2 * i + q, :, 128 + 128 * p : 256 + 128 * p] for i in range(rows)],
                    axis=0,
                )
                skips += dot(fine, grad_decoder[p, q], TN)
                through = dot(grad_decoder[p, q], skip[...], NT)
                for i in range(rows):
                    partial[2 * i + q, :, p * 128 : (p + 1) * 128] = through[
                        i * width : (i + 1) * width
                    ]
        skip_term[...] = skips
        before[:, width : width + 8, :] = jnp.zeros((2 * rows, 8, 128), jnp.float32)
        for i in range(rows):
            here = slice(i * width, (i + 1) * width)
            even = backs[1][here]
            odd = backs[2][here]
            if i + 1 < rows:
                odd = odd + backs[0][(i + 1) * width : (i + 2) * width]
            for q, line in enumerate((even, odd)):
                before[2 * i + q, 0:width, :] = line[:, 0:128]
                partial[2 * i + q, :, 0:128] += line[:, 128:256]
                partial[2 * i + q, :, 128:256] += (
                    line[:, 256:384] + before[2 * i + q, 1 : width + 1, :]
                )
        edge[...] = before[:, 0:1, :]


def back(left, gradient, right, weight, pooled, up, slope2, taps, grads, skip, weight2, context):
    rows, width = gradient.shape[0], gradient.shape[1]
    pixels = rows * width
    bf16, f32 = jnp.bfloat16, jnp.float32
    operands = (
        left, gradient, right, weight, pooled, up, slope2, taps, grads, skip, weight2, context,
    )
    specs = [whole(x.shape) for x in operands]
    specs[3] = pl.BlockSpec((1, *weight.shape[1:]), lambda n: (n, 0, 0))
    outs = [
        jax.ShapeDtypeStruct((2 * rows, width, 256), f32),
        jax.ShapeDtypeStruct((2 * rows, 1, 128), f32),
        jax.ShapeDtypeStruct((3, 384, 256), f32),
        jax.ShapeDtypeStruct((256, 128), f32),
        jax.ShapeDtypeStruct((128, 128), f32),
    ]
    return pl.pallas_call(
        back_kernel,
        out_shape=outs,
        grid=(TAPS,),
        in_specs=specs,
        out_specs=[whole(x.shape) for x in outs],
        scratch_shapes=[
            pltpu.VMEM((rows, width + 96, 256), bf16),
            pltpu.VMEM((pixels, 256), f32),
            pltpu.VMEM((2 * rows, width + 8, 128), f32),
        ],
        compiler_params=params(56),
        cost_estimate=LIGHT,
        name="back",
    )(*operands)


def finish_kernel(
    partial, returned, slope1, image, halo, term2, up_term, skip_term, out_term, out, packed, shifted_up
):
    rows, width = partial.shape[0], partial.shape[1]
    last = lax.broadcasted_iota(jnp.int32, (rows, width, 128), 1) == width - 1
    even = partial[:, :, 0:128]
    odd = partial[:, :, 128:256] + jnp.where(last, returned[...], 0.0)
    for i in range(rows):
        out[i, pl.ds(0, width, stride=2), :] = even[i]
        out[i, pl.ds(1, width, stride=2), :] = odd[i]
    even = even * slope1[:, :, 0:128]
    odd = (odd * slope1[:, :, 128:256]).astype(jnp.bfloat16)
    shifted_up[:, 0:16, :] = jnp.zeros((rows, 16, 128), jnp.float32)
    shifted_up[:, width + 8 : width + 16, :] = jnp.zeros((rows, 8, 128), jnp.float32)
    shifted_up[:, 15 : 15 + width, :] = even
    even = even.astype(jnp.bfloat16)
    moved = shifted_up[...].astype(jnp.bfloat16)
    rhs = jnp.concatenate([odd, even, moved[:, 16:]], axis=2)
    for a in range(3):
        first = 1 if a == 0 else 0
        lines = [2 * i + a - 1 for i in range(first, rows)]
        lhs = jnp.concatenate([image[n] for n in lines], axis=0)
        result = dot(lhs, rhs[first:].reshape((rows - first) * width, 384), TN)
        side = jnp.concatenate([halo[n] for n in lines], axis=0)
        outer = dot(side, moved[first:, 0:16].reshape((rows - first) * 16, 128), TN)
        at = 192 * a
        packed[at : at + 64, :] = (
            result[192:256, 256:384] + outer[192:256] + result[64:128, 0:128]
        )
        packed[at + 64 : at + 128, :] = result[0:64, 128:256] + result[128:192, 0:128]
        packed[at + 128 : at + 192, :] = result[64:128, 128:256] + result[192:256, 0:128]
        for n in range(2):
            at = 576 + 384 * (2 * a + n)
            packed[at : at + 384, :] = term2[a, :, n * 128 : (n + 1) * 128]
    packed[2880:3136, :] = up_term[...]
    packed[3136:3264, :] = skip_term[...]
    packed[3264:3272, :] = out_term[...]
    packed[3272:, :] = jnp.zeros((packed.shape[0] - 3272, 128), jnp.float32)


def finish(partial, returned, slope1, image, halo, terms, packed_rows):
    rows, width = partial.shape[0], partial.shape[1]
    f32 = jnp.float32
    return pl.pallas_call(
        finish_kernel,
        out_shape=[
            jax.ShapeDtypeStruct((rows, 2 * width, 128), f32),
            jax.ShapeDtypeStruct((packed_rows, 128), f32),
        ],
        in_specs=[VMEM] * 9,
        out_specs=[VMEM] * 2,
        scratch_shapes=[pltpu.VMEM((rows, width + 16, 128), f32)],
        compiler_params=params(56),
        cost_estimate=LIGHT,
        name="finish",
    )(partial, returned, slope1, image, halo, *terms)


def moved(block, distance):
    tiles = lax.axis_size("tile")
    route = [(i, i + distance) for i in range(tiles) if 0 <= i + distance < tiles]
    return lax.ppermute(block, "tile", route)


def edges(value):
    return moved(value[:, -48:], 1), moved(value[:, :48], -1)


def body(
    scan_pixels,
    labels,
    conv1_weight,
    conv2_weight,
    context_weight,
    up_weight,
    skip_weight,
    class_weight,
):
    bf16 = jnp.bfloat16
    tiles = lax.axis_size("tile")
    chips = tiles // 2
    t, _, half = position()
    place = jnp.stack([t, half]).astype(jnp.int32)
    lines, line_pairs, _ = scan_pixels[0].shape
    rows, width = lines // 4, line_pairs // 2
    corner = moved(scan_pixels[0, :, -2:, :].reshape(lines, 1, 256), 1)
    halo = jnp.concatenate([jnp.zeros((lines, 15, 256), bf16), corner], axis=1)
    image = scan_pixels[0].reshape(lines, width, 256)
    taps, slope1, features, slope2 = encode(image, halo, conv1_weight, conv2_weight)
    left, right = edges(features)
    logits, gradient, mine, theirs, context, pooled, grads, out_term = decode(
        place, left, features, right, context_weight, taps, labels[0],
        up_weight, skip_weight, class_weight, chips,
    )
    messages = pack(place, features, mine, flip(theirs, 1, 0))
    gradient, messages = lax.optimization_barrier((gradient, messages))

    def send(m, message):
        return flip(message, 2 * (m % chips), m // chips)

    own = [messages[0]] + [send(m, messages[m]) for m in range(1, 2 * chips)]
    left, right = edges(gradient)
    partial, edge, conv2_term, up_term, skip_term = back(
        left, gradient, right, context_weight, pooled, up_weight, slope2, taps, grads,
        skip_weight, conv2_weight, context,
    )
    returned = moved(edge, -1)
    partial, own = lax.optimization_barrier((partial, own))
    other = [flip(part, 1, 0) for part in own]
    packed_rows = -(-3272 // (64 * chips)) * 64 * chips
    grad_features, packed = finish(
        partial, returned, slope1, image, halo,
        (conv2_term, up_term, skip_term, out_term), packed_rows,
    )
    other, packed = lax.optimization_barrier((other, packed))
    block = mine.shape[2]
    context_term = wgrad(place, own, other, chips, rows, width, block)
    logits = logits.reshape(2, 2, K, rows, width).transpose(2, 3, 1, 4, 0)
    logits = logits.reshape(1, K, 2 * rows, 2 * width)
    grad_features = grad_features[None]
    scale = 1.0 / (lax.axis_size("dp") * tiles * 4 * rows * width)
    folded, context_term = fold_small(packed, chips, context_term)
    grad_context, small, logits = sum_and_share(
        context_term, folded, place, chips, block, scale, logits, packed_rows
    )
    return (
        logits,
        grad_features,
        small[0],
        small[1],
        grad_context.reshape(context_weight.shape),
        small[2],
        small[3],
        small[4],
    )


def solution(mesh):
    in_specs = (P("dp", None, "tile", None), P("dp", None, "tile"), P(), P(), P(), P(), P(), P())
    out_specs = (
        P("dp", None, None, "tile"),
        P("dp", None, "tile", None),
        P(),
        P(),
        P(),
        P(),
        P(),
        P(),
    )
    return jax.shard_map(body, mesh=mesh, in_specs=in_specs, out_specs=out_specs, check_vma=False)
```
